128 devices in a mesh: batch: 8 (over y_hi, x), task: 16 (over y_lo, z, core).
Axes of the slice: x: 4, y: 4 (y_hi: 2, y_lo: 2; y = y_hi * 2 + y_lo), z: 4, core: 2. Of those that a mesh axis runs over, the one named last changes fastest.
Arguments:
- x_quant: bfloat16 [4096, 4096], P('batch', 'task'), may hold values from -6 to 6
- x_scale: bfloat16 [4096, 32], P('batch', 'task'), may hold values from 0.25 to 2.5
- user_feats: bfloat16 [4096, 384], P('batch'), may hold values from -6 to 6
- scenario_ids: int32 [4096], P('batch'), may hold values from 0 to 31
- scenario_table: bfloat16 [32, 128], replicated, may hold values from -6 to 6
- label_mask: int32 [4096, 16], P('batch', 'task'), may hold values 0 or 1
- saved_z: bfloat16 [16, 4096, 2048], P('task', 'batch'), may hold values from -6 to 6
- out_grad: bfloat16 [16, 4096, 2048], P('task', 'batch'), may hold values from -4 to 4
- main_weight: bfloat16 [16, 4096, 2048], P('task'), may hold values from -0.09375 to 0.09375
- gate_a: bfloat16 [16, 512, 512], P('task'), may hold values from -0.25 to 0.25
- gate_b: bfloat16 [16, 512, 2048], P('task'), may hold values from -0.25 to 0.25
Outputs:
- main_grad: bfloat16 [16, 4096, 2048], P('task', 'batch')
- gate_a_grad: bfloat16 [16, 512, 512], P('task', 'batch')
- gate_b_grad: bfloat16 [16, 512, 2048], P('task', 'batch')
- x_grad: bfloat16 [4096, 4096], P('batch', 'task')
- user_grad: bfloat16 [4096, 384], P('batch', 'task')
- table_grad: float32 [32, 128], replicated
The draws below stay inside these ranges and needn't reach their ends.
All inputs are finite; a program needn't handle non-finite values. No bound on the sum of `label_mask` on one device may be relied on, other than what follows from the above.
Results may differ from the reference program's by a relative error of at most 0.02.
Values may be sent and summed in bfloat16 or wider, within the bound.
A program may use at most 192 MiB of HBM per device.

```python
import math
import jax
import jax.numpy as jnp
from jax import lax

D = 4096
H = 2048
GH = 512
UD = 384
SE = 128
NSCEN = 32
BLK = 128
TOK_DEV = 512
TOKENS = 4096
TOWERS = 16
GIN = 512
N_BATCH = 8


def set_ends(result, own_key, low, top_value):
    longest = result.shape.index(max(result.shape))
    spots = []
    for shift in (0, 1):
        where = [jax.random.randint(jax.random.fold_in(own_key, axis), (), 0, length) for axis, length in enumerate(result.shape)]
        where[longest] = (where[longest] + shift) % result.shape[longest]
        spots.append(tuple(where))
    return result.at[spots[0]].set(low).at[spots[1]].set(top_value)


def with_spikes(result, rng, source, target, parts, factor):
    owner, partner = [(jnp.arange(result.shape[position]) // (result.shape[position] // parts)).reshape([-1 if axis == position else 1 for axis in range(result.ndim)]) for position in (source, target)]
    chosen = jax.random.permutation(rng, parts)[partner]
    strong = (owner == chosen) | (owner == (partner + parts // 2) % parts)
    return jnp.where(strong, factor * result, result)


def block_levels(own_key, extent, shards, low, top_value):
    def one(position, blocks):
        heights = jax.random.uniform(jax.random.fold_in(jax.random.fold_in(own_key, 6), position), (blocks,), jnp.float32, low / len(shards), top_value / len(shards))
        return jnp.repeat(jnp.exp(heights), extent[position] // blocks).reshape((-1,) + (1,) * (len(extent) - position - 1))

    loudness = one(*shards[0])
    for cut in shards[1:]:
        loudness = loudness * one(*cut)
    return loudness


def bell_draw(stream_key, extent, scale, limit, cuts=(), kind=jnp.bfloat16):
    array = scale * jax.random.normal(stream_key, extent, jnp.float32)
    if cuts:
        array = array * block_levels(stream_key, extent, cuts, -0.22, 0.18)
    return jnp.clip(array, -limit, limit).astype(kind)


def bell_draw_with(key, shape, spread, most, shards, heavy, kind=jnp.bfloat16):
    array = spread * jax.random.normal(key, shape, jnp.float32)
    if shards:
        array = array * block_levels(key, shape, shards, -0.22, 0.18)
    return jnp.clip(with_spikes(array, jax.random.fold_in(key, 3), *heavy), -most, most).astype(kind)


def setup_inputs(seed: int = 0) -> dict:
    splits = jax.random.split(jax.random.key(seed), 12)
    x_quant = bell_draw_with(splits[0], (TOKENS, D), 1.0, 6.0, ((0, 8), (1, 16)), (0, 1, 16, 2.0))
    x_scale = jnp.clip(jnp.exp(math.log(2.5) - 2.3025851 * jax.random.uniform(splits[1], (TOKENS, D // BLK), jnp.float32) ** block_levels(splits[1], (TOKENS, D // BLK), ((0, 8), (1, 16)), -0.2, 0.2)), 0.25, 2.5).astype(jnp.bfloat16)
    user_feats = bell_draw(splits[2], (TOKENS, UD), 1.0, 6.0, ((0, 8),))
    scenario_ids = set_ends(jax.random.randint(splits[3], (TOKENS,), 0, NSCEN), jax.random.fold_in(splits[3], 1), 0, NSCEN - 1).astype(jnp.int32)
    scenario_table = bell_draw(splits[4], (NSCEN, SE), 1.0, 6.0)
    label_mask = set_ends((jax.random.randint(splits[5], (TOKENS, TOWERS), 0, 2) < 1).astype(jnp.int32), jax.random.fold_in(splits[5], 1), 0, 1)
    saved_z = bell_draw(splits[6], (TOWERS, TOKENS, H), 1.0, 6.0, ((0, 16), (1, 8)))
    out_grad = bell_draw(splits[7], (TOWERS, TOKENS, H), 0.25, 4.0, ((0, 16), (1, 8)))
    main_weight = bell_draw(splits[8], (TOWERS, D, H), D ** -0.5, 0.09375, ((0, 16),))
    gate_a = bell_draw(splits[9], (TOWERS, GIN, GH), GIN ** -0.5, 0.25, ((0, 16),))
    gate_b = bell_draw(splits[10], (TOWERS, GH, H), GH ** -0.5, 0.25, ((0, 16),))
    return dict(x_quant=x_quant, x_scale=x_scale, user_feats=user_feats, scenario_ids=scenario_ids, scenario_table=scenario_table, label_mask=label_mask, saved_z=saved_z, out_grad=out_grad, main_weight=main_weight, gate_a=gate_a, gate_b=gate_b)


def dequantize(values, scales):
    row_count, width = values.shape
    blocks = scales.shape[1]
    grid = values.astype(jnp.float32).reshape(row_count, blocks, width // blocks) * scales.astype(jnp.float32)[:, :, None]
    return grid.reshape(row_count, width).astype(jnp.bfloat16)


def batch_sum(left_side, right_side):
    left_parts = left_side.reshape(N_BATCH, TOK_DEV, left_side.shape[1])
    right_parts = right_side.reshape(N_BATCH, TOK_DEV, right_side.shape[1])

    def add_member(running, portion):
        partial_value = jnp.dot(portion[0].T, portion[1], preferred_element_type=jnp.float32)
        rounded = lax.optimization_barrier(partial_value.astype(jnp.bfloat16))
        return running + rounded.astype(jnp.float32), None

    start_sum = jnp.zeros((left_side.shape[1], right_side.shape[1]), jnp.float32)
    running, _ = lax.scan(add_member, start_sum, (left_parts, right_parts))
    return running.astype(jnp.bfloat16)


def reference(x_quant, x_scale, user_feats, scenario_ids, scenario_table, label_mask, saved_z, out_grad, main_weight, gate_a, gate_b):
    inputs = dequantize(x_quant, x_scale)
    onehot = (scenario_ids[:, None] == jnp.arange(NSCEN, dtype=jnp.int32)[None, :]).astype(jnp.bfloat16)
    scen_rows = jnp.dot(onehot, scenario_table, preferred_element_type=jnp.float32).astype(jnp.bfloat16)
    gate_in = jnp.concatenate([user_feats, scen_rows], axis=1)

    def tower(carry, stacked):
        weight, weight_a, weight_b, preact_saved, grad_above, mask_column = stacked
        a_pre = jnp.dot(gate_in, weight_a, preferred_element_type=jnp.float32)
        a_act = jnp.maximum(a_pre, 0.0).astype(jnp.bfloat16)
        gate_value = 2.0 * jax.nn.sigmoid(jnp.dot(a_act, weight_b, preferred_element_type=jnp.float32))
        masked = grad_above.astype(jnp.float32) * mask_column.astype(jnp.float32)[:, None]
        preact = preact_saved.astype(jnp.float32)
        z_grad = (masked * gate_value * (preact > 0)).astype(jnp.bfloat16)
        u_grad = (masked * jnp.maximum(preact, 0.0) * gate_value * (1.0 - 0.5 * gate_value)).astype(jnp.bfloat16)
        a_back = jnp.dot(u_grad, weight_b.T, preferred_element_type=jnp.float32)
        a_grad = (a_back * (a_pre > 0)).astype(jnp.bfloat16)
        gin_grad = jnp.dot(a_grad, weight_a.T, preferred_element_type=jnp.float32)
        x_part = jnp.dot(z_grad, weight.T, preferred_element_type=jnp.float32)
        main_part = batch_sum(inputs, z_grad)
        a_part = batch_sum(gate_in, a_grad)
        b_part = batch_sum(a_act, u_grad)
        x_total, gin_total = carry
        return (x_total + x_part, gin_total + gin_grad), (main_part, a_part, b_part)

    start_carry = (jnp.zeros((TOKENS, D), jnp.float32), jnp.zeros((TOKENS, GIN), jnp.float32))
    (x_total, gin_total), (main_grad, gate_a_grad, gate_b_grad) = lax.scan(
        tower, start_carry, (main_weight, gate_a, gate_b, saved_z, out_grad, label_mask.T))
    table_grad = jnp.einsum('rc,rs->cs', onehot.astype(jnp.float32), gin_total[:, UD:], precision=lax.Precision.HIGHEST)
    return (main_grad, gate_a_grad, gate_b_grad, x_total.astype(jnp.bfloat16),
            gin_total[:, :UD].astype(jnp.bfloat16), table_grad)
```

```python
import jax
import jax.numpy as jnp
from jax import lax
from jax.experimental import pallas as pl
from jax.experimental.pallas import tpu as pltpu
from jax.sharding import PartitionSpec as P

MESH = pl.DeviceIdType.MESH
F32 = jnp.float32
BF16 = jnp.bfloat16

ROWS = 512
H = 2048
GH = 512
UD = 384
CH = 256
STEPS = H // CH
XB = 288
USER = 24

Z_Y, Z_E0, Z_FW = 0, 8, 16
G_E1, G_Y, G_E0 = 24, 33, 34
I_PERM, I_YL, I_Z1, I_Z2, I_CORE = 35, 36, 37, 39, 41
M_E1 = 45
X_CORE, X_Z1, X_Z2, X_YL = 53, 61, 63, 67
T_ALL = 68
N_SEM = 75


def nt(a, b):
    return lax.dot_general(a, b, (((1,), (1,)), ((), ())), preferred_element_type=F32)


def nn(a, b):
    return jnp.dot(a, b, preferred_element_type=F32)


def kernel(
    xq, xs, feats, ids_col, ids_row, table, mask_col, ga, gb, sz_hbm, og_hbm, w_hbm,
    main_out, ga_out, gb_out, x_out, user_out, table_out,
    sz, og, wbuf, zall, gin_in, act, a_back, gint, aall, x_own,
    gpart, gr1, gr2, gr3, xsend, xkeep, xcore, xz1, xz2, xylsend, xyl, ps, pr, tsend, trecv,
    lsem, ssem, rsem,
):
    bi = lax.axis_index("batch")
    ti = lax.axis_index("task")
    yh, x = bi // 4, bi % 4
    yl, z, c = ti // 8, (ti // 2) % 4, ti % 2
    x0 = x + 1 - 2 * (x % 2)
    x1 = 3 - x
    xp = x // 2
    z0 = z + 1 - 2 * (z % 2)

    def dev(yh_, x_, yl_, z_, c_):
        return (yh_ * 4 + x_, yl_ * 8 + z_ * 2 + c_)

    d_y = dev(1 - yh, x, yl, z, c)
    d_e0 = dev(yh, x0, yl, z, c)
    d_e1 = dev(yh, x1, yl, z, c)
    d_c = dev(yh, x, yl, z, 1 - c)
    d_yl = dev(yh, x, 1 - yl, z, c)
    d_zp = dev(yh, x, yl, (z + 1) % 4, c)
    d_zm = dev(yh, x, yl, (z + 3) % 4, c)
    member = jnp.logical_or(z == x, z == 3 - x)
    ksel = jnp.where(member, 0, 1)
    is_self = jnp.logical_and(member, yh == yl)
    d_perm = dev(yl, x + ksel * (x0 - x), yh, z + ksel * (z0 - z), c)

    def rcopy(src, dst, i, target):
        return pltpu.make_async_remote_copy(
            src_ref=src, dst_ref=dst, send_sem=ssem.at[i], recv_sem=rsem.at[i],
            device_id=target, device_id_type=MESH)

    def send(src, dst, i, target):
        rcopy(src, dst, i, target).start()

    def got(ref, i):
        rcopy(ref, ref, i, d_c).wait_recv()

    def sent(ref, i):
        rcopy(ref, ref, i, d_c).wait_send()

    def cols(k):
        return pl.ds(pl.multiple_of(k * CH, CH), CH)

    def wcopy(k):
        return pltpu.make_async_copy(
            w_hbm.at[pl.ds(pl.multiple_of(k * 512, 512), 512)], wbuf.at[k % 2], lsem.at[2 + k % 2])

    sz_copy = pltpu.make_async_copy(sz_hbm, sz, lsem.at[0])
    og_copy = pltpu.make_async_copy(og_hbm, og, lsem.at[1])
    sz_copy.start()
    og_copy.start()
    wcopy(0).start()
    wcopy(1).start()

    barrier = pltpu.get_barrier_semaphore()
    for target in (d_y, d_e0, d_e1, d_c, d_yl, d_zp, d_zm):
        pl.semaphore_signal(barrier, inc=1, device_id=target, device_id_type=MESH)

    @pl.when(jnp.logical_not(is_self))
    def _():
        pl.semaphore_signal(barrier, inc=1, device_id=d_perm, device_id_type=MESH)

    half = xq.shape[1] // 2
    for j in range(2):
        part = xq[:, j * half:(j + 1) * half].astype(F32) * xs[:, j:j + 1].astype(F32)
        x_own[j * half:(j + 1) * half, :] = part.T.astype(BF16)

    pl.semaphore_wait(barrier, jnp.where(is_self, 7, 8))

    def place(zz, core, first, count):
        d_ = jnp.where(zz // 2 == xp, 1, 0)
        k_ = jnp.where(jnp.logical_or(zz == x, zz == 3 - x), 0, 1)
        off = pl.multiple_of((k_ * 2 + first) * ROWS, ROWS)
        return aall.at[d_, core, :, pl.ds(off, count * ROWS)]

    @pl.when(is_self)
    def _():
        local = pltpu.make_async_copy(x_own, place(z, c, yl, 1), lsem.at[4])
        local.start()
        local.wait()

    @pl.when(jnp.logical_not(is_self))
    def _():
        send(x_own, place(z, c, yh, 1), I_PERM, d_perm)

    onehot = (ids_col[...] == lax.broadcasted_iota(jnp.int32, (ROWS, 32), 1)).astype(BF16)
    gin_in[:, :UD] = feats[...]
    gin_in[:, UD:] = nn(onehot, table[...]).astype(BF16)
    a_pre = nn(gin_in[...], ga[...])
    a_act = jnp.maximum(a_pre, 0.0)
    act[0] = a_act.astype(BF16)
    act[1] = a_act.T.astype(BF16)
    a_back[...] = jnp.zeros_like(a_back)
    mask = mask_col[...].astype(F32)
    sz_copy.wait()
    og_copy.wait()

    def first(k, carry):
        cc = cols(k)
        gate = 2.0 * jax.nn.sigmoid(nn(act[0], gb[:, cc]))
        masked = og[:, cc].astype(F32) * mask
        pre = sz[:, cc].astype(F32)
        mg = masked * gate
        zall[yh, :, cc] = jnp.where(pre > 0, mg, 0.0).astype(BF16)
        send(zall.at[yh, :, cc], zall.at[yh, :, cc], Z_Y + k, d_y)

        @pl.when(k < 4)
        def _():
            send(zall.at[yh, :, cc], zall.at[2 + yh, :, cc], Z_E0 + k, d_e0)

        u = (jnp.maximum(pre, 0.0) * mg * (1.0 - 0.5 * gate)).astype(BF16)
        part = nn(act[1], u).astype(BF16)
        for i in range(2):
            for j in range(2):
                r = (i * 2 + j) * 128
                gpart[i, j, :, cc] = part[r:r + 128]
        send(gpart.at[:, 1 - xp, :, cc], gr1.at[:, :, cc], G_E1 + k, d_e1)
        a_back[...] += nt(u, gb[:, cc])
        return carry

    lax.fori_loop(0, STEPS, first, 0)

    @pl.when(jnp.logical_not(is_self))
    def _():
        got(place(z, c, yl, 1), I_PERM)

    send(place(z, c, yl, 1), place(z, c, yl, 1), I_YL, d_yl)

    a_grad = jnp.where(act[0].astype(F32) > 0, a_back[...], 0.0).astype(BF16)
    part = nn(gin_in[...].astype(F32).T.astype(BF16), a_grad).astype(BF16)
    for i in range(2):
        for j in range(2):
            r = (i * 2 + j) * 128
            gpart[i, j, :, H:] = part[r:r + 128]
    send(gpart.at[:, 1 - xp, :, pl.ds(H, GH)], gr1.at[:, :, pl.ds(H, GH)], G_E1 + 8, d_e1)
    gint[...] = nt(ga[...], a_grad)
    scen = nt(a_grad, ga[UD:, :])
    onehot_t = (ids_row[...] == lax.broadcasted_iota(jnp.int32, (32, ROWS), 0)).astype(F32)
    tsend[0] = lax.dot_general(
        onehot_t, scen, (((1,), (0,)), ((), ())), precision=lax.Precision.HIGHEST, preferred_element_type=F32)
    t_partners = (d_c, d_e0, d_yl, dev(yh, x, yl, z0, c), d_e1, dev(yh, x, yl, 3 - z, c), d_y)
    send(tsend.at[0], trecv.at[0], T_ALL, t_partners[0])

    def user_rows(t):
        rows = gint[pl.ds(pl.multiple_of(t * USER, 8), USER), :]
        return jnp.concatenate([rows, jnp.zeros((XB - 256 - USER, ROWS), F32)], axis=0).astype(BF16)

    def second(k, carry):
        cc = cols(k)
        wcopy(k).wait()
        wrows = wbuf.at[k % 2]
        other = 1 - c
        own_z = zall[yh]
        xsend[k, :256, :] = nt(wrows[pl.ds(pl.multiple_of(other * 256, 256), 256), :], own_z).astype(BF16)
        xsend[k, 256:, :] = user_rows(k * 2 + other)
        send(xsend.at[k], xcore.at[k], X_CORE + k, d_c)
        xkeep[k, :256, :] = nt(wrows[pl.ds(pl.multiple_of(c * 256, 256), 256), :], own_z).astype(BF16)
        xkeep[k, 256:, :] = user_rows(k * 2 + c)

        @pl.when(k < STEPS - 2)
        def _():
            wcopy(k + 2).start()

        got(zall.at[1 - yh, :, cc], Z_Y + k)
        send(zall.at[1 - yh, :, cc], zall.at[3 - yh, :, cc], Z_FW + k, d_e0)

        @pl.when(k < 4)
        def _():
            more = cols(k + 4)
            send(zall.at[yh, :, more], zall.at[2 + yh, :, more], Z_E0 + 4 + k, d_e0)

        for s in range(1, 7):

            @pl.when(k == s)
            def _():
                got(trecv.at[s - 1], T_ALL + s - 1)
                tsend[s] = tsend[s - 1] + trecv[s - 1]
                send(tsend.at[s], trecv.at[s], T_ALL + s, t_partners[s])

        @pl.when(k == 1)
        def _():
            got(place(z, c, 1 - yl, 1), I_YL)
            mine = place(z, c, 0, 2)
            send(mine, mine, I_Z1, d_zp)
            send(mine, mine, I_Z1 + 1, d_zm)
            send(mine, mine, I_CORE, d_c)

        @pl.when(k == 4)
        def _():
            got(place((z + 3) % 4, c, 0, 2), I_Z1)
            got(place((z + 1) % 4, c, 0, 2), I_Z1 + 1)
            low = place((z + 3) % 4, c, 0, 1)
            send(low, low, I_Z2, d_zp)
            high = place((z + 1) % 4, c, 1, 1)
            send(high, high, I_Z2 + 1, d_zm)
            for i, zz in ((1, (z + 3) % 4), (2, (z + 1) % 4)):
                mine = place(zz, c, 0, 2)
                send(mine, mine, I_CORE + i, d_c)

        @pl.when(k == 6)
        def _():
            got(place((z + 2) % 4, c, 0, 1), I_Z2)
            got(place((z + 2) % 4, c, 1, 1), I_Z2 + 1)
            mine = place((z + 2) % 4, c, 0, 2)
            send(mine, mine, I_CORE + 3, d_c)

        return carry

    lax.fori_loop(0, STEPS, second, 0)

    got(trecv.at[6], T_ALL + 6)
    table_out[...] = tsend[6] + trecv[6]

    def core_sum(k, carry):
        got(xcore.at[k], X_CORE + k)
        xkeep[k] = (xkeep[k].astype(F32) + xcore[k].astype(F32)).astype(BF16)
        return carry

    lax.fori_loop(0, STEPS, core_sum, 0)
    zn, zb, zf = (z + 1) % 4, (z + 3) % 4, (z + 2) % 4
    send(xkeep.at[zf], xz1.at[0], X_Z1, d_zp)
    send(xkeep.at[4 + zf], xz1.at[1], X_Z1 + 1, d_zm)

    for k in range(STEPS):
        got(gr1.at[:, :, pl.ds(k * CH, CH)], G_E1 + k)
    got(gr1.at[:, :, pl.ds(H, GH)], G_E1 + 8)
    gpart[1 - yh, xp] = (gpart[1 - yh, xp].astype(F32) + gr1[1 - yh].astype(F32)).astype(BF16)
    send(gpart.at[1 - yh, xp], gr2, G_Y, d_y)

    for i, zz in enumerate((zb, zn, zf)):
        got(place(zz, 1 - c, 0, 2), I_CORE + 1 + i)
    got(place(z, 1 - c, 0, 2), I_CORE)

    def third(k, carry):
        @pl.when(k < STEPS)
        def _():
            cc = cols(k)
            got(zall.at[2 + yh, :, cc], Z_E0 + k)
            got(zall.at[3 - yh, :, cc], Z_FW + k)
            for j in range(2):
                total = nn(aall[0, j, :, 0:ROWS], zall[0, :, cc])
                for s in range(1, 4):
                    total += nn(aall[0, j, :, s * ROWS:(s + 1) * ROWS], zall[s, :, cc])
                ps[j * 256:(j + 1) * 256, cc] = total.astype(BF16)
            send(ps.at[:, cc], pr.at[:, cc], M_E1 + k, d_e1)

        @pl.when(k >= 1)
        def _():
            cc = cols(k - 1)
            got(pr.at[:, cc], M_E1 + k - 1)
            for j in range(2):
                total = pr[j * 256:(j + 1) * 256, cc].astype(F32)
                for s in range(4):
                    total += nn(aall[1, j, :, s * ROWS:(s + 1) * ROWS], zall[s, :, cc])
                main_out[j * 256:(j + 1) * 256, cc] = total.astype(BF16)

        @pl.when(k == 1)
        def _():
            got(xz1.at[0], X_Z1)
            got(xz1.at[1], X_Z1 + 1)
            xkeep[zn] = (xkeep[zn].astype(F32) + xz1[0].astype(F32)).astype(BF16)
            xkeep[4 + zb] = (xkeep[4 + zb].astype(F32) + xz1[1].astype(F32)).astype(BF16)
            for h in range(2):
                send(xkeep.at[h * 4 + zn], xz2.at[0, h], X_Z2 + 2 * h, d_zp)
                send(xkeep.at[h * 4 + zb], xz2.at[1, h], X_Z2 + 1 + 2 * h, d_zm)

        @pl.when(k == 2)
        def _():
            got(gr2, G_Y)
            gpart[yh, xp] = (
                gpart[yh, xp].astype(F32) + gr1[yh].astype(F32) + gr2[...].astype(F32)).astype(BF16)
            far = pl.ds(pl.multiple_of((x0 % 2) * 64, 64), 64)
            send(gpart.at[yh, xp, far], gr3, G_E0, d_e0)

        @pl.when(k == 4)
        def _():
            for h in range(2):
                got(xz2.at[0, h], X_Z2 + 2 * h)
                got(xz2.at[1, h], X_Z2 + 1 + 2 * h)
            xylsend[...] = (
                xkeep[(1 - yl) * 4 + z].astype(F32) + xz2[0, 1 - yl].astype(F32) + xz2[1, 1 - yl].astype(F32)
            ).astype(BF16)
            send(xylsend, xyl, X_YL, d_yl)

        @pl.when(k == 6)
        def _():
            got(gr3, G_E0)
            near = pl.ds(pl.multiple_of((x % 2) * 64, 64), 64)
            total = gpart[yh, xp, near, :].astype(F32) + gr3[...].astype(F32)
            gb_out[...] = total[:, :H].astype(BF16)
            ga_out[...] = total[:, H:].astype(BF16)

        @pl.when(k == 7)
        def _():
            got(xyl, X_YL)
            total = (
                xkeep[yl * 4 + z].astype(F32) + xz2[0, yl].astype(F32) + xz2[1, yl].astype(F32)
                + xyl[...].astype(F32))
            x_out[...] = total[:256].T.astype(BF16)
            user_out[...] = total[256:].T.astype(BF16)

        return carry

    lax.fori_loop(0, STEPS + 1, third, 0)

    def drain(k, carry):
        cc = cols(k)
        sent(zall.at[0, :, cc], Z_Y + k)
        sent(zall.at[0, :, cc], Z_E0 + k)
        sent(zall.at[0, :, cc], Z_FW + k)
        sent(gr1.at[:, :, cc], G_E1 + k)
        sent(ps.at[:, cc], M_E1 + k)
        sent(xsend.at[k], X_CORE + k)
        return carry

    lax.fori_loop(0, STEPS, drain, 0)
    sent(gr1.at[:, :, pl.ds(H, GH)], G_E1 + 8)
    sent(gr2, G_Y)
    sent(gr3, G_E0)

    @pl.when(jnp.logical_not(is_self))
    def _():
        sent(x_own, I_PERM)

    sent(place(z, c, 0, 1), I_YL)
    for i in range(2):
        sent(place(z, c, 0, 2), I_Z1 + i)
        sent(place(z, c, 0, 1), I_Z2 + i)
        sent(xz1.at[i], X_Z1 + i)
    for i in range(4):
        sent(place(z, c, 0, 2), I_CORE + i)
        sent(xz2.at[0, 0], X_Z2 + i)
    sent(xyl, X_YL)
    for s in range(7):
        sent(tsend.at[s], T_ALL + s)


def body(
    x_quant, x_scale, user_feats, scenario_ids, scenario_table, label_mask,
    saved_z, out_grad, main_weight, gate_a, gate_b,
):
    vmem = pl.BlockSpec(memory_space=pltpu.VMEM)
    hbm = pl.BlockSpec(memory_space=pl.ANY)
    outs = pl.pallas_call(
        kernel,
        out_shape=(
            jax.ShapeDtypeStruct((512, H), BF16),
            jax.ShapeDtypeStruct((64, GH), BF16),
            jax.ShapeDtypeStruct((64, H), BF16),
            jax.ShapeDtypeStruct((ROWS, 256), BF16),
            jax.ShapeDtypeStruct((ROWS, 32), BF16),
            jax.ShapeDtypeStruct((32, 128), F32),
        ),
        in_specs=[vmem] * 9 + [hbm] * 3,
        out_specs=(vmem,) * 6,
        scratch_shapes=[
            pltpu.VMEM((ROWS, H), BF16),
            pltpu.VMEM((ROWS, H), BF16),
            pltpu.VMEM((2, 512, H), BF16),
            pltpu.VMEM((4, ROWS, H), BF16),
            pltpu.VMEM((ROWS, GH), BF16),
            pltpu.VMEM((2, ROWS, GH), BF16),
            pltpu.VMEM((ROWS, GH), F32),
            pltpu.VMEM((512, ROWS), F32),
            pltpu.VMEM((2, 2, 256, 4 * ROWS), BF16),
            pltpu.VMEM((256, ROWS), BF16),
            pltpu.VMEM((2, 2, 128, H + GH), BF16),
            pltpu.VMEM((2, 128, H + GH), BF16),
            pltpu.VMEM((128, H + GH), BF16),
            pltpu.VMEM((64, H + GH), BF16),
            pltpu.VMEM((8, XB, ROWS), BF16),
            pltpu.VMEM((8, XB, ROWS), BF16),
            pltpu.VMEM((8, XB, ROWS), BF16),
            pltpu.VMEM((2, XB, ROWS), BF16),
            pltpu.VMEM((2, 2, XB, ROWS), BF16),
            pltpu.VMEM((XB, ROWS), BF16),
            pltpu.VMEM((XB, ROWS), BF16),
            pltpu.VMEM((512, H), BF16),
            pltpu.VMEM((512, H), BF16),
            pltpu.VMEM((7, 32, 128), F32),
            pltpu.VMEM((7, 32, 128), F32),
            pltpu.SemaphoreType.DMA((5,)),
            pltpu.SemaphoreType.DMA((N_SEM,)),
            pltpu.SemaphoreType.DMA((N_SEM,)),
        ],
        compiler_params=pltpu.CompilerParams(
            collective_id=0, has_side_effects=True, vmem_limit_bytes=60 * 1024 * 1024),
        cost_estimate=pl.CostEstimate(flops=21_000_000_000, bytes_accessed=28_000_000, transcendentals=1_000_000),
    )(
        x_quant, x_scale, user_feats, scenario_ids[:, None], scenario_ids[None, :], scenario_table,
        label_mask, gate_a[0], gate_b[0], saved_z[0], out_grad[0], main_weight[0],
    )
    main, grad_a, grad_b, x_grad, user, table_grad = outs
    return main[None], grad_a[None], grad_b[None], x_grad, user[:, :USER], table_grad


def solution(mesh):
    placed = (
        P("batch", "task"),
        P("batch", "task"),
        P("batch", None),
        P("batch"),
        P(),
        P("batch", "task"),
        P("task", "batch", None),
        P("task", "batch", None),
        P("task", None, None),
        P("task", None, None),
        P("task", None, None),
    )
    return jax.shard_map(
        body,
        mesh=mesh,
        in_specs=placed,
        out_specs=(
            P("task", "batch", None),
            P("task", "batch", None),
            P("task", "batch", None),
            P("batch", "task"),
            P("batch", "task"),
            P(),
        ),
        check_vma=False,
    )
```

```python
import jax
import jax.numpy as jnp
from jax import lax
from jax.experimental import pallas as pl
from jax.experimental.pallas import tpu as pltpu
from jax.sharding import PartitionSpec as P

MESH = pl.DeviceIdType.MESH
F32 = jnp.float32
BF16 = jnp.bfloat16

ROWS = 512
H = 2048
GH = 512
UD = 384
CH = 256
STEPS = H // CH
XB = 288
USER = 24
CAP = 320
DEPTH = 4 * CAP
LAG = 3

Z_Y, Z_E0, Z_FW = 0, 8, 16
G_E1, G_Y, G_E0 = 24, 33, 34
I_PERM, I_YL, I_Z1, I_Z2, I_CORE = 35, 36, 37, 41, 45
M_E1 = 49
X_CORE, X_Z1, X_Z2, X_YL = 57, 65, 67, 71
T_ALL = 72
S_ALL = 79
N_SEM = 82


def nt(a, b):
    return lax.dot_general(a, b, (((1,), (1,)), ((), ())), preferred_element_type=F32)


def nn(a, b):
    return jnp.dot(a, b, preferred_element_type=F32)


def kernel(
    xq, xs, feats, ids, table, mask_in, ga, gb, sz_hbm, og_hbm, w_hbm,
    main_out, ga_out, gb_out, x_out, user_out, table_out, flag_out,
    sz, og, wbuf, zfull, zc, gin_in, act, a_back, gint, aall, ac, x_own, pick, sel,
    gpart, gr1, gr2, gr3, xsend, xkeep, xcore, xz1, xz2, xylsend, xyl, ps, pr, tsend, trecv,
    lsem, ssem, rsem,
):
    bi = lax.axis_index("batch")
    ti = lax.axis_index("task")
    yh, x = bi // 4, bi % 4
    yl, z, c = ti // 8, (ti // 2) % 4, ti % 2
    x0 = x + 1 - 2 * (x % 2)
    x1 = 3 - x
    xp = x // 2
    z0 = z + 1 - 2 * (z % 2)

    def dev(yh_, x_, yl_, z_, c_):
        return (yh_ * 4 + x_, yl_ * 8 + z_ * 2 + c_)

    d_y = dev(1 - yh, x, yl, z, c)
    d_e0 = dev(yh, x0, yl, z, c)
    d_e1 = dev(yh, x1, yl, z, c)
    d_c = dev(yh, x, yl, z, 1 - c)
    d_yl = dev(yh, x, 1 - yl, z, c)
    d_zp = dev(yh, x, yl, (z + 1) % 4, c)
    d_zm = dev(yh, x, yl, (z + 3) % 4, c)
    member = jnp.logical_or(z == x, z == 3 - x)
    ksel = jnp.where(member, 0, 1)
    is_self = jnp.logical_and(member, yh == yl)
    d_diag = dev(1 - yh, x0, yl, z, c)
    d_perm = dev(yl, x + ksel * (x0 - x), yh, z + ksel * (z0 - z), c)

    def rcopy(src, dst, i, target):
        return pltpu.make_async_remote_copy(
            src_ref=src, dst_ref=dst, send_sem=ssem.at[i], recv_sem=rsem.at[i],
            device_id=target, device_id_type=MESH)

    def send(src, dst, i, target):
        rcopy(src, dst, i, target).start()

    def got(ref, i):
        rcopy(ref, ref, i, d_c).wait_recv()

    def sent(ref, i):
        rcopy(ref, ref, i, d_c).wait_send()

    def packed(s):
        return pl.ds(pl.multiple_of(s * CAP, CAP), CAP)

    def cols(k):
        return pl.ds(pl.multiple_of(k * CH, CH), CH)

    def wcopy(k):
        return pltpu.make_async_copy(
            w_hbm.at[pl.ds(pl.multiple_of(k * 512, 512), 512)], wbuf.at[k % 2], lsem.at[2 + k % 2])

    sz_copy = pltpu.make_async_copy(sz_hbm, sz, lsem.at[0])
    og_copy = pltpu.make_async_copy(og_hbm, og, lsem.at[1])
    sz_copy.start()
    og_copy.start()
    wcopy(0).start()
    wcopy(1).start()

    barrier = pltpu.get_barrier_semaphore()
    for target in (d_y, d_e0, d_e1, d_c, d_yl, d_zp, d_zm, d_diag):
        pl.semaphore_signal(barrier, inc=1, device_id=target, device_id_type=MESH)

    @pl.when(jnp.logical_not(is_self))
    def _():
        pl.semaphore_signal(barrier, inc=1, device_id=d_perm, device_id_type=MESH)

    half = xq.shape[1] // 2
    for j in range(2):
        part = xq[:, j * half:(j + 1) * half].astype(F32).T * xs[j:j + 1, :].astype(F32)
        x_own[j * half:(j + 1) * half, :] = part.astype(BF16)

    mask_row = jnp.broadcast_to(mask_in[...], (8, ROWS)).astype(F32)
    before = (
        lax.broadcasted_iota(jnp.int32, (ROWS, ROWS), 0) < lax.broadcasted_iota(jnp.int32, (ROWS, ROWS), 1)
    ).astype(BF16)
    rank = nn(mask_row.astype(BF16), before)
    sel[yh] = jnp.where(mask_row > 0, rank, -1.0)

    def picker(s):
        return (
            lax.broadcasted_iota(jnp.int32, (CAP, ROWS), 0).astype(F32) == sel[s, 0:1, :]
        ).astype(BF16)

    pick[...] = picker(yh)

    pl.semaphore_wait(barrier, jnp.where(is_self, 8, 9))

    def place(zz, core, first, count):
        d_ = jnp.where(zz // 2 == xp, 1, 0)
        k_ = jnp.where(jnp.logical_or(zz == x, zz == 3 - x), 0, 1)
        off = pl.multiple_of((k_ * 2 + first) * ROWS, ROWS)
        return aall.at[d_, core, :, pl.ds(off, count * ROWS)]

    @pl.when(is_self)
    def _():
        local = pltpu.make_async_copy(x_own, place(z, c, yl, 1), lsem.at[4])
        local.start()
        local.wait()

    @pl.when(jnp.logical_not(is_self))
    def _():
        send(x_own, place(z, c, yh, 1), I_PERM, d_perm)

    send(sel.at[yh], sel.at[yh], S_ALL, d_y)
    send(sel.at[yh], sel.at[2 + yh], S_ALL + 1, d_e0)
    send(sel.at[yh], sel.at[2 + yh], S_ALL + 2, d_diag)

    onehot_t = (ids[...] == lax.broadcasted_iota(jnp.int32, (32, ROWS), 0)).astype(F32)
    gin_in[:, :UD] = feats[...]
    gin_in[:, UD:] = nn(onehot_t.T.astype(BF16), table[...]).astype(BF16)
    a_pre = nn(gin_in[...], ga[...])
    a_act = jnp.maximum(a_pre, 0.0)
    act[0] = a_act.astype(BF16)
    act[1] = a_act.T.astype(BF16)
    a_back[...] = jnp.zeros_like(a_back)
    mask = mask_row.T[:, 0:1]
    sz_copy.wait()
    og_copy.wait()

    def first(k, carry):
        cc = cols(k)
        gate = 2.0 * jax.nn.sigmoid(nn(act[0], gb[:, cc]))
        masked = og[:, cc].astype(F32) * mask
        pre = sz[:, cc].astype(F32)
        mg = masked * gate
        zk = jnp.where(pre > 0, mg, 0.0).astype(BF16)
        zfull[:, cc] = zk
        zc[packed(yh), cc] = nn(pick[...], zk).astype(BF16)

        @pl.when(k < 4)
        def _():
            send(zc.at[packed(yh), cc], zc.at[packed(2 + yh), cc], Z_E0 + k, d_e0)

        @pl.when(k == 5)
        def _():
            @pl.when(jnp.logical_not(is_self))
            def _():
                got(place(z, c, yl, 1), I_PERM)

            mine = place(z, c, yl, 1)
            send(mine, mine, I_YL, d_yl)
            send(mine, mine, I_Z1, d_zp)
            send(mine, mine, I_Z1 + 1, d_zm)

            def early(n, carry):
                send(zc.at[packed(yh), cols(n)], zc.at[packed(yh), cols(n)], Z_Y + n, d_y)
                return carry

            lax.fori_loop(0, 5, early, 0)

        @pl.when(k >= 5)
        def _():
            send(zc.at[packed(yh), cc], zc.at[packed(yh), cc], Z_Y + k, d_y)

        u = (jnp.maximum(pre, 0.0) * mg * (1.0 - 0.5 * gate)).astype(BF16)
        part = nn(act[1], u).astype(BF16)
        for i in range(2):
            for j in range(2):
                r = (i * 2 + j) * 128
                gpart[i, j, :, cc] = part[r:r + 128]
        send(gpart.at[:, 1 - xp, :, cc], gr1.at[:, :, cc], G_E1 + k, d_e1)
        a_back[...] += nt(u, gb[:, cc])
        return carry

    lax.fori_loop(0, STEPS, first, 0)

    a_grad = jnp.where(act[0].astype(F32) > 0, a_back[...], 0.0).astype(BF16)
    part = nn(gin_in[...].astype(F32).T.astype(BF16), a_grad).astype(BF16)
    for i in range(2):
        for j in range(2):
            r = (i * 2 + j) * 128
            gpart[i, j, :, H:] = part[r:r + 128]
    send(gpart.at[:, 1 - xp, :, pl.ds(H, GH)], gr1.at[:, :, pl.ds(H, GH)], G_E1 + 8, d_e1)
    gint[...] = nt(ga[...], a_grad)
    scen = nt(a_grad, ga[UD:, :])
    tsend[0, :32] = lax.dot_general(
        onehot_t, scen, (((1,), (0,)), ((), ())), precision=lax.Precision.HIGHEST, preferred_element_type=F32)
    over = jnp.maximum(jnp.sum(mask_row, axis=1, keepdims=True) - CAP, 0.0)
    tsend[0, 32:] = jnp.broadcast_to(over, (8, 128))
    t_partners = (d_c, dev(yh, x, yl, z0, c), dev(yh, x, yl, 3 - z, c), d_yl, d_y, d_e1, d_e0)
    send(tsend.at[0], trecv.at[0], T_ALL, t_partners[0])

    def user_rows(t):
        rows = gint[pl.ds(pl.multiple_of(t * USER, 8), USER), :]
        return jnp.concatenate([rows, jnp.zeros((XB - 256 - USER, ROWS), F32)], axis=0).astype(BF16)

    zn, zb, zf = (z + 1) % 4, (z + 3) % 4, (z + 2) % 4

    def half_rows(zz, first, h):
        d_ = jnp.where(zz // 2 == xp, 1, 0)
        k_ = jnp.where(jnp.logical_or(zz == x, zz == 3 - x), 0, 1)
        off = pl.multiple_of((k_ * 2 + first) * ROWS, ROWS)
        return aall.at[d_, c, pl.ds(h * 128, 128), pl.ds(off, ROWS)]

    def z_forward(n, first):
        got(place(zb, c, first, 1), I_Z1 + 2 * n)
        got(place(zn, c, first, 1), I_Z1 + 2 * n + 1)
        low, high = half_rows(zb, first, 0), half_rows(zn, first, 1)
        send(low, low, I_Z2 + 2 * n, d_zp)
        send(high, high, I_Z2 + 2 * n + 1, d_zm)

    def to_core(zz, i):
        mine = place(zz, c, 0, 2)
        send(mine, mine, I_CORE + i, d_c)

    def x_block(k, carry):
        wcopy(k).wait()
        wrows = wbuf.at[k % 2]
        other = 1 - c
        xsend[k, :256, :] = nt(wrows[pl.ds(pl.multiple_of(other * 256, 256), 256), :], zfull[...]).astype(BF16)
        xsend[k, 256:, :] = user_rows(k * 2 + other)
        send(xsend.at[k], xcore.at[k], X_CORE + k, d_c)
        xkeep[k, :256, :] = nt(wrows[pl.ds(pl.multiple_of(c * 256, 256), 256), :], zfull[...]).astype(BF16)
        xkeep[k, 256:, :] = user_rows(k * 2 + c)

        @pl.when(k < STEPS - 2)
        def _():
            wcopy(k + 2).start()

        return carry

    def second(k):
        cc = cols(k)

        @pl.when(k < 4)
        def _():
            lax.fori_loop(2 * k, 2 * k + 2, x_block, 0)

        @pl.when(k == 0)
        def _():
            got(place(z, c, 1 - yl, 1), I_YL)
            mine = place(z, c, 1 - yl, 1)
            send(mine, mine, I_Z1 + 2, d_zp)
            send(mine, mine, I_Z1 + 3, d_zm)
            to_core(z, 0)
            z_forward(0, yl)

        @pl.when(k == 1)
        def _():
            z_forward(1, 1 - yl)
            to_core(zb, 1)
            to_core(zn, 2)

        @pl.when(k == 2)
        def _():
            for n, first in enumerate((yl, 1 - yl)):
                got(half_rows(zf, first, 0), I_Z2 + 2 * n)
                got(half_rows(zf, first, 1), I_Z2 + 2 * n + 1)
            to_core(zf, 3)

        got(zc.at[packed(1 - yh), cc], Z_Y + k)
        send(zc.at[packed(1 - yh), cc], zc.at[packed(3 - yh), cc], Z_FW + k, d_e0)

        @pl.when(k < 4)
        def _():
            more = cols(k + 4)
            send(zc.at[packed(yh), more], zc.at[packed(2 + yh), more], Z_E0 + 4 + k, d_e0)

    def table_step(s):
        got(trecv.at[s - 1], T_ALL + s - 1)
        tsend[s] = tsend[s - 1] + trecv[s - 1]
        send(tsend.at[s], trecv.at[s], T_ALL + s, t_partners[s])

    def pack_inputs():
        for i, zz in enumerate((z, zb, zn, zf)):
            got(place(zz, 1 - c, 0, 2), I_CORE + i)
        got(sel.at[1 - yh], S_ALL)
        got(sel.at[2 + yh], S_ALL + 1)
        got(sel.at[3 - yh], S_ALL + 2)
        for s in range(4):
            p = picker(s)
            for d_ in range(2):
                for j in range(2):
                    ac[d_, j, :, s * CAP:(s + 1) * CAP] = nt(
                        aall[d_, j, :, s * ROWS:(s + 1) * ROWS], p).astype(BF16)

    def core_sum():
        def one(n, carry):
            got(xcore.at[n], X_CORE + n)
            xkeep[n] = (xkeep[n].astype(F32) + xcore[n].astype(F32)).astype(BF16)
            return carry

        lax.fori_loop(0, STEPS, one, 0)
        send(xkeep.at[zf], xz1.at[0], X_Z1, d_zp)
        send(xkeep.at[4 + zf], xz1.at[1], X_Z1 + 1, d_zm)

    def gate_e1():
        for n in range(STEPS):
            got(gr1.at[:, :, pl.ds(n * CH, CH)], G_E1 + n)
        got(gr1.at[:, :, pl.ds(H, GH)], G_E1 + 8)
        gpart[1 - yh, xp] = (gpart[1 - yh, xp].astype(F32) + gr1[1 - yh].astype(F32)).astype(BF16)
        send(gpart.at[1 - yh, xp], gr2, G_Y, d_y)

    def gate_y():
        got(gr2, G_Y)
        gpart[yh, xp] = (
            gpart[yh, xp].astype(F32) + gr1[yh].astype(F32) + gr2[...].astype(F32)).astype(BF16)
        far = pl.ds(pl.multiple_of((x0 % 2) * 64, 64), 64)
        send(gpart.at[yh, xp, far], gr3, G_E0, d_e0)

    def gate_e0():
        got(gr3, G_E0)
        near = pl.ds(pl.multiple_of((x % 2) * 64, 64), 64)
        total = gpart[yh, xp, near, :].astype(F32) + gr3[...].astype(F32)
        gb_out[...] = total[:, :H].astype(BF16)
        ga_out[...] = total[:, H:].astype(BF16)

    def x_z1():
        got(xz1.at[0], X_Z1)
        got(xz1.at[1], X_Z1 + 1)
        xkeep[zn] = (xkeep[zn].astype(F32) + xz1[0].astype(F32)).astype(BF16)
        xkeep[4 + zb] = (xkeep[4 + zb].astype(F32) + xz1[1].astype(F32)).astype(BF16)
        for h in range(2):
            send(xkeep.at[h * 4 + zn], xz2.at[0, h], X_Z2 + 2 * h, d_zp)
            send(xkeep.at[h * 4 + zb], xz2.at[1, h], X_Z2 + 1 + 2 * h, d_zm)

    def x_z2():
        for h in range(2):
            got(xz2.at[0, h], X_Z2 + 2 * h)
            got(xz2.at[1, h], X_Z2 + 1 + 2 * h)
        xylsend[...] = (
            xkeep[(1 - yl) * 4 + z].astype(F32) + xz2[0, 1 - yl].astype(F32) + xz2[1, 1 - yl].astype(F32)
        ).astype(BF16)
        send(xylsend, xyl, X_YL, d_yl)

    def x_last():
        got(xyl, X_YL)
        total = (
            xkeep[yl * 4 + z].astype(F32) + xz2[0, yl].astype(F32) + xz2[1, yl].astype(F32)
            + xyl[...].astype(F32))
        x_out[...] = total[:256].T.astype(BF16)
        user_out[...] = total[256:256 + USER].astype(BF16)

    def table_last():
        got(trecv.at[6], T_ALL + 6)
        total = tsend[6] + trecv[6]
        table_out[...] = total[:32]
        flag_out[0, 0] = total[32, 0]

    def table_at(s):
        return lambda: table_step(s)

    extra = {
        1: (table_at(1),),
        3: (table_at(2),),
        4: (core_sum,),
        5: (table_at(3), x_z1, gate_e1),
        7: (table_at(4),),
        8: (table_at(5), x_z2),
        9: (table_at(6), gate_y),
        10: (x_last,),
        11: (table_last, gate_e0),
    }

    def step(i, carry):
        @pl.when(i < STEPS)
        def _():
            second(i)

        @pl.when(i == LAG)
        def _():
            pack_inputs()

        j = i - LAG

        @pl.when(jnp.logical_and(j >= 0, j < STEPS))
        def _():
            cc = cols(j)
            got(zc.at[packed(2 + yh), cc], Z_E0 + j)
            got(zc.at[packed(3 - yh), cc], Z_FW + j)
            for h in range(2):
                ps[h * 256:(h + 1) * 256, cc] = nn(ac[0, h], zc[:, cc]).astype(BF16)
            send(ps.at[:, cc], pr.at[:, cc], M_E1 + j, d_e1)

        for at, calls in extra.items():

            @pl.when(i == at)
            def _():
                for call in calls:
                    call()

        @pl.when(jnp.logical_and(j >= 1, j <= STEPS))
        def _():
            cc = cols(j - 1)
            got(pr.at[:, cc], M_E1 + j - 1)
            for h in range(2):
                total = pr[h * 256:(h + 1) * 256, cc].astype(F32) + nn(ac[1, h], zc[:, cc])
                main_out[h * 256:(h + 1) * 256, cc] = total.astype(BF16)

        return carry

    lax.fori_loop(0, STEPS + LAG + 1, step, 0)

    def drain(k, carry):
        cc = cols(k)
        sent(zc.at[packed(0), cc], Z_Y + k)
        sent(zc.at[packed(0), cc], Z_E0 + k)
        sent(zc.at[packed(0), cc], Z_FW + k)
        sent(gr1.at[:, :, cc], G_E1 + k)
        sent(ps.at[:, cc], M_E1 + k)
        sent(xsend.at[k], X_CORE + k)
        return carry

    lax.fori_loop(0, STEPS, drain, 0)
    sent(gr1.at[:, :, pl.ds(H, GH)], G_E1 + 8)
    sent(gr2, G_Y)
    sent(gr3, G_E0)

    @pl.when(jnp.logical_not(is_self))
    def _():
        sent(x_own, I_PERM)

    sent(place(z, c, 0, 1), I_YL)
    for i in range(4):
        sent(place(z, c, 0, 1), I_Z1 + i)
        sent(half_rows(z, 0, 0), I_Z2 + i)
    for i in range(2):
        sent(xz1.at[i], X_Z1 + i)
    for i in range(3):
        sent(sel.at[0], S_ALL + i)
    for i in range(4):
        sent(place(z, c, 0, 2), I_CORE + i)
        sent(xz2.at[0, 0], X_Z2 + i)
    sent(xyl, X_YL)
    for s in range(7):
        sent(tsend.at[s], T_ALL + s)


def copy_kernel(*refs):
    n = len(refs) // 2
    for i in range(n):
        refs[n + i][...] = refs[i][...]


def copy_out(*arrays):
    vmem = pl.BlockSpec(memory_space=pltpu.VMEM)
    return pl.pallas_call(
        copy_kernel,
        out_shape=tuple(jax.ShapeDtypeStruct(a.shape, a.dtype) for a in arrays),
        in_specs=[vmem] * len(arrays),
        out_specs=(vmem,) * len(arrays),
    )(*arrays)


def main_grad_wide(
    x_quant, x_scale, user_feats, scenario_ids, scenario_table, label_mask, saved_z, out_grad, gate_a, gate_b,
):
    onehot = (scenario_ids[:, None] == jnp.arange(32, dtype=jnp.int32)[None, :]).astype(BF16)
    scen_rows = jnp.dot(onehot, scenario_table, preferred_element_type=F32).astype(BF16)
    gate_in = jnp.concatenate([user_feats, scen_rows], axis=1)
    a_act = jnp.maximum(jnp.dot(gate_in, gate_a[0], preferred_element_type=F32), 0.0).astype(BF16)
    gate = 2.0 * jax.nn.sigmoid(jnp.dot(a_act, gate_b[0], preferred_element_type=F32))
    masked = out_grad[0].astype(F32) * label_mask.astype(F32)
    z_grad = (masked * gate * (saved_z[0] > 0)).astype(BF16)
    blocks = x_scale.shape[1]
    own = (
        x_quant.astype(F32).reshape(ROWS, blocks, -1) * x_scale.astype(F32)[:, :, None]
    ).reshape(ROWS, -1).astype(BF16)
    inputs = lax.all_to_all(jnp.broadcast_to(own, (16, *own.shape)), "task", 0, 0)
    partial = jnp.einsum("trd,rh->tdh", inputs, z_grad, preferred_element_type=F32).astype(BF16)
    parts = lax.all_to_all(partial.reshape(8, 512, H), "batch", 0, 0)
    return jnp.sum(parts.astype(F32), axis=0).astype(BF16)


def body(
    x_quant, x_scale, user_feats, scenario_ids, scenario_table, label_mask,
    saved_z, out_grad, main_weight, gate_a, gate_b,
):
    vmem = pl.BlockSpec(memory_space=pltpu.VMEM)
    hbm = pl.BlockSpec(memory_space=pl.ANY)
    outs = pl.pallas_call(
        kernel,
        out_shape=(
            jax.ShapeDtypeStruct((512, H), BF16),
            jax.ShapeDtypeStruct((64, GH), BF16),
            jax.ShapeDtypeStruct((64, H), BF16),
            jax.ShapeDtypeStruct((ROWS, 256), BF16),
            jax.ShapeDtypeStruct((USER, ROWS), BF16),
            jax.ShapeDtypeStruct((32, 128), F32),
            jax.ShapeDtypeStruct((1, 1), F32),
        ),
        in_specs=[vmem] * 8 + [hbm] * 3,
        out_specs=(vmem,) * 6 + (pl.BlockSpec(memory_space=pltpu.SMEM),),
        scratch_shapes=[
            pltpu.VMEM((ROWS, H), BF16),
            pltpu.VMEM((ROWS, H), BF16),
            pltpu.VMEM((2, 512, H), BF16),
            pltpu.VMEM((ROWS, H), BF16),
            pltpu.VMEM((DEPTH, H), BF16),
            pltpu.VMEM((ROWS, GH), BF16),
            pltpu.VMEM((2, ROWS, GH), BF16),
            pltpu.VMEM((ROWS, GH), F32),
            pltpu.VMEM((512, ROWS), F32),
            pltpu.VMEM((2, 2, 256, 4 * ROWS), BF16),
            pltpu.VMEM((2, 2, 256, DEPTH), BF16),
            pltpu.VMEM((256, ROWS), BF16),
            pltpu.VMEM((CAP, ROWS), BF16),
            pltpu.VMEM((4, 8, ROWS), F32),
            pltpu.VMEM((2, 2, 128, H + GH), BF16),
            pltpu.VMEM((2, 128, H + GH), BF16),
            pltpu.VMEM((128, H + GH), BF16),
            pltpu.VMEM((64, H + GH), BF16),
            pltpu.VMEM((8, XB, ROWS), BF16),
            pltpu.VMEM((8, XB, ROWS), BF16),
            pltpu.VMEM((8, XB, ROWS), BF16),
            pltpu.VMEM((2, XB, ROWS), BF16),
            pltpu.VMEM((2, 2, XB, ROWS), BF16),
            pltpu.VMEM((XB, ROWS), BF16),
            pltpu.VMEM((XB, ROWS), BF16),
            pltpu.VMEM((512, H), BF16),
            pltpu.VMEM((512, H), BF16),
            pltpu.VMEM((7, 40, 128), F32),
            pltpu.VMEM((7, 40, 128), F32),
            pltpu.SemaphoreType.DMA((5,)),
            pltpu.SemaphoreType.DMA((N_SEM,)),
            pltpu.SemaphoreType.DMA((N_SEM,)),
        ],
        compiler_params=pltpu.CompilerParams(
            collective_id=0, has_side_effects=True, vmem_limit_bytes=60 * 1024 * 1024),
        cost_estimate=pl.CostEstimate(flops=21_000_000_000, bytes_accessed=28_000_000, transcendentals=1_000_000),
    )(
        x_quant, x_scale.T, user_feats, scenario_ids[None, :], scenario_table,
        label_mask.T, gate_a[0], gate_b[0], saved_z[0], out_grad[0], main_weight[0],
    )
    main, grad_a, grad_b, x_grad, user, table_grad = copy_out(*outs[:6])
    args = (
        x_quant, x_scale, user_feats, scenario_ids, scenario_table, label_mask, saved_z, out_grad, gate_a, gate_b)
    _, main = lax.while_loop(
        lambda carry: carry[0] > 0,
        lambda carry: (jnp.zeros_like(carry[0]), main_grad_wide(*args)),
        (outs[6][0, 0], main))
    return main[None], grad_a[None], grad_b[None], x_grad, user.T, table_grad


def solution(mesh):
    placed = (
        P("batch", "task"),
        P("batch", "task"),
        P("batch", None),
        P("batch"),
        P(),
        P("batch", "task"),
        P("task", "batch", None),
        P("task", "batch", None),
        P("task", None, None),
        P("task", None, None),
        P("task", None, None),
    )
    return jax.shard_map(
        body,
        mesh=mesh,
        in_specs=placed,
        out_specs=(
            P("task", "batch", None),
            P("task", "batch", None),
            P("task", "batch", None),
            P("batch", "task"),
            P("batch", "task"),
            P(),
        ),
        check_vma=False,
    )
```

```python
import functools

import jax
import jax.numpy as jnp
from jax import lax
from jax.experimental import pallas as pl
from jax.experimental.pallas import tpu as pltpu
from jax.sharding import PartitionSpec as P

MESH = pl.DeviceIdType.MESH
F32 = jnp.float32
BF16 = jnp.bfloat16

ROWS = 512
H = 2048
GH = 512
UD = 384
CH = 256
STEPS = H // CH
XB = 288
USER = 24
CAP = 320
DEPTH = 4 * CAP
FIRST = 6
AHEAD = 2
LAG = 2

Z_Y, Z_E0, Z_FW = 0, 8, 16
G_E1, G_Y, G_E0 = 24, 33, 34
I_PERM, I_YL, I_Z1, I_Z2, I_CORE = 35, 37, 39, 47, 51
M_E1 = 55
X_CORE, X_Z1, X_Z2, X_YL = 63, 71, 73, 77
T_ALL = 78
S_ALL = 85
I_WAY = 88
N_SEM = 90


def nt(a, b):
    return lax.dot_general(a, b, (((1,), (1,)), ((), ())), preferred_element_type=F32)


def nn(a, b):
    return jnp.dot(a, b, preferred_element_type=F32)


def kernel(
    xs, ids, table, mask_in, xq_hbm, feats_hbm, ga_hbm, gb_hbm, sz_hbm, og_hbm, w_hbm,
    main_out, ga_out, gb_out, x_out, user_out, table_out, flag_out,
    xq, feats, ga, gb, sz, og, wbuf, zfull, zc, gin_in, act, a_back, gint, aall, ac, x_own, x_way, pick, sel,
    gpart, gr1, gr2, gr3, xsend, xkeep, xcore, xz1, xz2, xylsend, xyl, ps, pr, main_v, tsend, trecv,
    lsem, ssem, rsem,
):
    bi = lax.axis_index("batch")
    ti = lax.axis_index("task")
    yh, x = bi // 4, bi % 4
    yl, z, c = ti // 8, (ti // 2) % 4, ti % 2
    x0 = x + 1 - 2 * (x % 2)
    x1 = 3 - x
    xp = x // 2
    z0 = z + 1 - 2 * (z % 2)

    def dev(yh_, x_, yl_, z_, c_):
        return (yh_ * 4 + x_, yl_ * 8 + z_ * 2 + c_)

    d_y = dev(1 - yh, x, yl, z, c)
    d_e0 = dev(yh, x0, yl, z, c)
    d_e1 = dev(yh, x1, yl, z, c)
    d_c = dev(yh, x, yl, z, 1 - c)
    d_yl = dev(yh, x, 1 - yl, z, c)
    d_zp = dev(yh, x, yl, (z + 1) % 4, c)
    d_zm = dev(yh, x, yl, (z + 3) % 4, c)
    member = jnp.logical_or(z == x, z == 3 - x)
    moved = jnp.logical_not(member)
    turn = yh != yl
    d_diag = dev(1 - yh, x0, yl, z, c)
    d_xz = dev(yh, x0, yl, z0, c)
    d_turn = dev(yl, x, yh, z, c)

    def rcopy(src, dst, i, target):
        return pltpu.make_async_remote_copy(
            src_ref=src, dst_ref=dst, send_sem=ssem.at[i], recv_sem=rsem.at[i],
            device_id=target, device_id_type=MESH)

    def send(src, dst, i, target):
        rcopy(src, dst, i, target).start()

    def got(ref, i):
        rcopy(ref, ref, i, d_c).wait_recv()

    def sent(ref, i):
        rcopy(ref, ref, i, d_c).wait_send()

    def packed(s):
        return pl.ds(pl.multiple_of(s * CAP, CAP), CAP)

    def cols(k):
        return pl.ds(pl.multiple_of(k * CH, CH), CH)

    def wcopy(k):
        return pltpu.make_async_copy(
            w_hbm.at[pl.ds(pl.multiple_of(k * 512, 512), 512)], wbuf.at[k % 2], lsem.at[2 + k % 2])

    loads = [
        pltpu.make_async_copy(src, dst, lsem.at[i]) for i, src, dst in (
            (5, xq_hbm, xq), (6, feats_hbm, feats), (7, ga_hbm, ga), (8, gb_hbm, gb), (0, sz_hbm, sz), (1, og_hbm, og))
    ]
    for load in loads:
        load.start()
    wcopy(0).start()
    wcopy(1).start()

    barrier = pltpu.get_barrier_semaphore()
    for target in (d_y, d_e0, d_e1, d_c, d_yl, d_zp, d_zm, d_diag):
        pl.semaphore_signal(barrier, inc=1, device_id=target, device_id_type=MESH)

    @pl.when(moved)
    def _():
        pl.semaphore_signal(barrier, inc=1, device_id=d_xz, device_id_type=MESH)

    @pl.when(turn)
    def _():
        pl.semaphore_signal(barrier, inc=1, device_id=d_turn, device_id_type=MESH)

    loads[0].wait()
    half = xq.shape[1] // 2
    for j in range(2):
        part = xq[:, j * half:(j + 1) * half].astype(F32).T * xs[j:j + 1, :].astype(F32)
        x_own[j * half:(j + 1) * half, :] = part.astype(BF16)

    mask_row = jnp.broadcast_to(mask_in[...], (8, ROWS)).astype(F32)
    before = (
        lax.broadcasted_iota(jnp.int32, (ROWS, ROWS), 0) < lax.broadcasted_iota(jnp.int32, (ROWS, ROWS), 1)
    ).astype(BF16)
    rank = nn(mask_row.astype(BF16), before)
    sel[yh] = jnp.where(mask_row > 0, rank, -1.0)

    def picker(s):
        return (
            lax.broadcasted_iota(jnp.int32, (CAP, ROWS), 0).astype(F32) == sel[s, 0:1, :]
        ).astype(BF16)

    pick[...] = picker(yh)

    pl.semaphore_wait(barrier, 8 + jnp.where(moved, 1, 0) + jnp.where(turn, 1, 0))

    def place(zz, core, first, count):
        d_ = jnp.where(zz // 2 == xp, 1, 0)
        k_ = jnp.where(jnp.logical_or(zz == x, zz == 3 - x), 0, 1)
        off = pl.multiple_of((k_ * 2 + first) * ROWS, ROWS)
        return aall.at[d_, core, :, pl.ds(off, count * ROWS)]

    def half_rows(zz, first, h):
        d_ = jnp.where(zz // 2 == xp, 1, 0)
        k_ = jnp.where(jnp.logical_or(zz == x, zz == 3 - x), 0, 1)
        off = pl.multiple_of((k_ * 2 + first) * ROWS, ROWS)
        return aall.at[d_, c, pl.ds(h * 128, 128), pl.ds(off, ROWS)]

    halves = [pl.ds(h * 128, 128) for h in range(2)]
    stays = jnp.logical_and(member, jnp.logical_not(turn))

    @pl.when(stays)
    def _():
        local = pltpu.make_async_copy(x_own, place(z, c, yl, 1), lsem.at[4])
        local.start()
        local.wait()

    @pl.when(jnp.logical_and(member, turn))
    def _():
        for h in range(2):
            send(x_own.at[halves[h]], half_rows(z, yh, h), I_PERM + h, d_turn)

    @pl.when(jnp.logical_and(moved, jnp.logical_not(turn)))
    def _():
        for h in range(2):
            send(x_own.at[halves[h]], half_rows(z, yl, h), I_PERM + h, d_xz)

    @pl.when(jnp.logical_and(moved, turn))
    def _():
        for h in range(2):
            send(x_own.at[halves[h]], x_way.at[halves[h]], I_WAY + h, d_xz)

    def turn_way(h):
        @pl.when(jnp.logical_and(moved, turn))
        def _():
            got(x_way.at[halves[h]], I_WAY + h)
            send(x_way.at[halves[h]], half_rows(z, yh, h), I_PERM + h, d_turn)

    send(sel.at[yh], sel.at[yh], S_ALL, d_y)
    send(sel.at[yh], sel.at[2 + yh], S_ALL + 1, d_e0)
    send(sel.at[yh], sel.at[2 + yh], S_ALL + 2, d_diag)

    onehot_t = (ids[...] == lax.broadcasted_iota(jnp.int32, (32, ROWS), 0)).astype(F32)
    for load in loads[1:]:
        load.wait()
    gin_in[:, :UD] = feats[...]
    gin_in[:, UD:] = nn(onehot_t.T.astype(BF16), table[...]).astype(BF16)
    a_pre = nn(gin_in[...], ga[...])
    a_act = jnp.maximum(a_pre, 0.0)
    act[0] = a_act.astype(BF16)
    act[1] = a_act.T.astype(BF16)
    a_back[...] = jnp.zeros_like(a_back)
    mask = mask_row.T[:, 0:1]

    def send_e0(n):
        send(zc.at[packed(yh), cols(n)], zc.at[packed(2 + yh), cols(n)], Z_E0 + n, d_e0)

    def first(k, carry):
        cc = cols(k)
        gate = 2.0 * jax.nn.sigmoid(nn(act[0], gb[:, cc]))
        masked = og[:, cc].astype(F32) * mask
        pre = sz[:, cc].astype(F32)
        mg = masked * gate
        zk = jnp.where(pre > 0, mg, 0.0).astype(BF16)
        zfull[:, cc] = zk
        zc[packed(yh), cc] = nn(pick[...], zk).astype(BF16)

        for h, at in enumerate((1, 3)):

            @pl.when(k == at)
            def _():
                turn_way(h)

        for h, at in enumerate((3, 5)):

            @pl.when(k == at)
            def _():
                mine = half_rows(z, yl, h)

                @pl.when(jnp.logical_not(stays))
                def _():
                    got(mine, I_PERM + h)

                send(mine, mine, I_YL + h, d_yl)
                send(mine, mine, I_Z1 + 2 * h, d_zp)
                send(mine, mine, I_Z1 + 2 * h + 1, d_zm)

        @pl.when(k < FIRST)
        def _():
            send_e0(k)

        u = (jnp.maximum(pre, 0.0) * mg * (1.0 - 0.5 * gate)).astype(BF16)
        part = nn(act[1], u).astype(BF16)
        for i in range(2):
            for j in range(2):
                r = (i * 2 + j) * 128
                gpart[i, j, :, cc] = part[r:r + 128]
        send(gpart.at[:, 1 - xp, :, cc], gr1.at[:, :, cc], G_E1 + k, d_e1)
        a_back[...] += nt(u, gb[:, cc])
        return carry

    lax.fori_loop(0, STEPS, first, 0)

    zn, zb, zf = (z + 1) % 4, (z + 3) % 4, (z + 2) % 4

    def z_low(n, first):
        low = half_rows(zb, first, 0)
        got(low, I_Z1 + 4 * n)
        send(low, low, I_Z2 + 2 * n, d_zp)

    def z_high(n, first):
        high = half_rows(zn, first, 1)
        got(high, I_Z1 + 4 * n + 3)
        send(high, high, I_Z2 + 2 * n + 1, d_zm)

    def z_rest(n, first):
        got(half_rows(zn, first, 0), I_Z1 + 4 * n + 1)
        got(half_rows(zb, first, 1), I_Z1 + 4 * n + 2)

    def to_core(zz, i):
        mine = place(zz, c, 0, 2)
        send(mine, mine, I_CORE + i, d_c)

    def from_y(h):
        near = half_rows(z, 1 - yl, h)
        got(near, I_YL + h)
        send(near, near, I_Z1 + 4 + 2 * h, d_zp)
        send(near, near, I_Z1 + 4 + 2 * h + 1, d_zm)

    def send_y(n, carry):
        send(zc.at[packed(yh), cols(n)], zc.at[packed(yh), cols(n)], Z_Y + n, d_y)
        return carry

    from_y(0)
    lax.fori_loop(0, 2, send_y, 0)
    z_low(0, yl)

    a_grad = jnp.where(act[0].astype(F32) > 0, a_back[...], 0.0).astype(BF16)
    part = nn(gin_in[...].astype(F32).T.astype(BF16), a_grad).astype(BF16)
    for i in range(2):
        for j in range(2):
            r = (i * 2 + j) * 128
            gpart[i, j, :, H:] = part[r:r + 128]
    send(gpart.at[:, 1 - xp, :, pl.ds(H, GH)], gr1.at[:, :, pl.ds(H, GH)], G_E1 + 8, d_e1)
    gint[...] = nt(ga[...], a_grad)
    scen = nt(a_grad, ga[UD:, :])
    tsend[0, :32] = lax.dot_general(
        onehot_t, scen, (((1,), (0,)), ((), ())), precision=lax.Precision.HIGHEST, preferred_element_type=F32)
    over = jnp.maximum(jnp.sum(mask_row, axis=1, keepdims=True) - CAP, 0.0)
    tsend[0, 32:] = jnp.broadcast_to(over, (8, 128))
    t_partners = (d_c, dev(yh, x, yl, z0, c), dev(yh, x, yl, 3 - z, c), d_e1, d_e0, d_yl, d_y)
    send(tsend.at[0], trecv.at[0], T_ALL, t_partners[0])

    def user_rows(t):
        rows = gint[pl.ds(pl.multiple_of(t * USER, 8), USER), :]
        return jnp.concatenate([rows, jnp.zeros((XB - 256 - USER, ROWS), F32)], axis=0).astype(BF16)

    from_y(1)

    lax.fori_loop(2, STEPS, send_y, 0)
    to_core(z, 0)
    z_high(0, yl)

    def x_block(k, carry):
        wcopy(k).wait()
        wrows = wbuf.at[k % 2]
        other = 1 - c
        xsend[k, :256, :] = nt(wrows[pl.ds(pl.multiple_of(other * 256, 256), 256), :], zfull[...]).astype(BF16)
        xsend[k, 256:, :] = user_rows(k * 2 + other)
        send(xsend.at[k], xcore.at[k], X_CORE + k, d_c)
        xkeep[k, :256, :] = nt(wrows[pl.ds(pl.multiple_of(c * 256, 256), 256), :], zfull[...]).astype(BF16)
        xkeep[k, 256:, :] = user_rows(k * 2 + c)

        @pl.when(k < STEPS - 2)
        def _():
            wcopy(k + 2).start()

        return carry

    def inputs_z2():
        for n, first in enumerate((yl, 1 - yl)):
            got(half_rows(zf, first, 0), I_Z2 + 2 * n)
            got(half_rows(zf, first, 1), I_Z2 + 2 * n + 1)
        to_core(zf, 3)

    def forward(k):
        cc = cols(k)
        got(zc.at[packed(1 - yh), cc], Z_Y + k)
        send(zc.at[packed(1 - yh), cc], zc.at[packed(3 - yh), cc], Z_FW + k, d_e0)

        @pl.when(jnp.logical_and(k >= 4, k < 6))
        def _():
            send_e0(k + 2)

    def table_step(s):
        got(trecv.at[s - 1], T_ALL + s - 1)
        tsend[s] = tsend[s - 1] + trecv[s - 1]
        send(tsend.at[s], trecv.at[s], T_ALL + s, t_partners[s])

    def wait_inputs():
        for i, zz in enumerate((z, zb, zn, zf)):
            got(place(zz, 1 - c, 0, 2), I_CORE + i)
        got(sel.at[1 - yh], S_ALL)
        got(sel.at[2 + yh], S_ALL + 1)
        got(sel.at[3 - yh], S_ALL + 2)

    def pack_inputs(d_):
        for s in range(4):
            p = picker(s)
            for j in range(2):
                ac[d_, j, :, s * CAP:(s + 1) * CAP] = nt(
                    aall[d_, j, :, s * ROWS:(s + 1) * ROWS], p).astype(BF16)

    def core_sum():
        def one(n, carry):
            got(xcore.at[n], X_CORE + n)
            xkeep[n] = (xkeep[n].astype(F32) + xcore[n].astype(F32)).astype(BF16)
            return carry

        lax.fori_loop(0, STEPS, one, 0)
        send(xkeep.at[zf], xz1.at[0], X_Z1, d_zp)
        send(xkeep.at[4 + zf], xz1.at[1], X_Z1 + 1, d_zm)

    def gate_e1():
        for n in range(STEPS):
            got(gr1.at[:, :, pl.ds(n * CH, CH)], G_E1 + n)
        got(gr1.at[:, :, pl.ds(H, GH)], G_E1 + 8)
        gpart[1 - yh, xp] = (gpart[1 - yh, xp].astype(F32) + gr1[1 - yh].astype(F32)).astype(BF16)
        send(gpart.at[1 - yh, xp], gr2, G_Y, d_y)

    def gate_y():
        got(gr2, G_Y)
        gpart[yh, xp] = (
            gpart[yh, xp].astype(F32) + gr1[yh].astype(F32) + gr2[...].astype(F32)).astype(BF16)
        far = pl.ds(pl.multiple_of((x0 % 2) * 64, 64), 64)
        send(gpart.at[yh, xp, far], gr3, G_E0, d_e0)

    def gate_e0():
        got(gr3, G_E0)
        near = pl.ds(pl.multiple_of((x % 2) * 64, 64), 64)
        total = gpart[yh, xp, near, :].astype(F32) + gr3[...].astype(F32)
        gb_out[...] = total[:, :H].astype(BF16)
        ga_out[...] = total[:, H:].astype(BF16)

    def x_z1():
        got(xz1.at[0], X_Z1)
        got(xz1.at[1], X_Z1 + 1)
        xkeep[zn] = (xkeep[zn].astype(F32) + xz1[0].astype(F32)).astype(BF16)
        xkeep[4 + zb] = (xkeep[4 + zb].astype(F32) + xz1[1].astype(F32)).astype(BF16)
        for h in range(2):
            send(xkeep.at[h * 4 + zn], xz2.at[0, h], X_Z2 + 2 * h, d_zp)
            send(xkeep.at[h * 4 + zb], xz2.at[1, h], X_Z2 + 1 + 2 * h, d_zm)

    def x_z2():
        for h in range(2):
            got(xz2.at[0, h], X_Z2 + 2 * h)
            got(xz2.at[1, h], X_Z2 + 1 + 2 * h)
        xylsend[...] = (
            xkeep[(1 - yl) * 4 + z].astype(F32) + xz2[0, 1 - yl].astype(F32) + xz2[1, 1 - yl].astype(F32)
        ).astype(BF16)
        send(xylsend, xyl, X_YL, d_yl)

    def x_last():
        got(xyl, X_YL)
        total = (
            xkeep[yl * 4 + z].astype(F32) + xz2[0, yl].astype(F32) + xz2[1, yl].astype(F32)
            + xyl[...].astype(F32))
        x_out[...] = total[:256].T.astype(BF16)
        user_out[...] = total[256:256 + USER].astype(BF16)

    def table_last():
        got(trecv.at[6], T_ALL + 6)
        total = tsend[6] + trecv[6]
        table_out[...] = total[:32]
        flag_out[0, 0] = total[32, 0]

    def table_at(s):
        return lambda: table_step(s)

    extra = {
        1: (table_at(1),),
        2: (table_at(2),),
        3: (core_sum, table_at(3)),
        5: (gate_e1,),
        6: (x_z1, table_at(4)),
        8: (table_at(5),),
        9: (x_z2, gate_y, table_at(6)),
        11: (x_last, gate_e0, table_last),
    }

    def main_copy(n):
        return pltpu.make_async_copy(main_v.at[:, cols(n)], main_out.at[:, cols(n)], lsem.at[9 + n])

    def step(i, carry):
        j = i - LAG

        @pl.when(i == 1)
        def _():
            forward(1)
            inputs_z2()

        @pl.when(i == LAG)
        def _():
            wait_inputs()
            pack_inputs(0)

        @pl.when(jnp.logical_and(j >= 0, j < STEPS))
        def _():
            cc = cols(j)
            got(zc.at[packed(2 + yh), cc], Z_E0 + j)
            got(zc.at[packed(3 - yh), cc], Z_FW + j)
            for h in range(2):
                ps[h * 256:(h + 1) * 256, cc] = nn(ac[0, h], zc[:, cc]).astype(BF16)
            send(ps.at[:, cc], pr.at[:, cc], M_E1 + j, d_e1)

        @pl.when(i == LAG)
        def _():
            pack_inputs(1)

        @pl.when(i < 4)
        def _():
            lax.fori_loop(2 * i, 2 * i + 2, x_block, 0)

        @pl.when(i == 0)
        def _():
            z_low(1, 1 - yl)
            z_high(1, 1 - yl)
            for n, first in enumerate((yl, 1 - yl)):
                z_rest(n, first)
            to_core(zb, 1)
            to_core(zn, 2)

        @pl.when(i < 2)
        def _():
            forward(2 * i)

        @pl.when(jnp.logical_and(i >= 2, i < 5))
        def _():
            forward(2 * i - 1)

            @pl.when(i < 4)
            def _():
                forward(2 * i)

        for at, calls in extra.items():

            @pl.when(i == at)
            def _():
                for call in calls:
                    call()

        @pl.when(j >= AHEAD)
        def _():
            cc = cols(j - AHEAD)
            got(pr.at[:, cc], M_E1 + j - AHEAD)
            for h in range(2):
                total = pr[h * 256:(h + 1) * 256, cc].astype(F32) + nn(ac[1, h], zc[:, cc])
                main_v[h * 256:(h + 1) * 256, cc] = total.astype(BF16)
            main_copy(j - AHEAD).start()

        return carry

    lax.fori_loop(0, STEPS + LAG + AHEAD, step, 0)

    def drain(k, carry):
        cc = cols(k)
        main_copy(k).wait()
        sent(zc.at[packed(0), cc], Z_Y + k)
        sent(zc.at[packed(0), cc], Z_E0 + k)
        sent(zc.at[packed(0), cc], Z_FW + k)
        sent(gr1.at[:, :, cc], G_E1 + k)
        sent(ps.at[:, cc], M_E1 + k)
        sent(xsend.at[k], X_CORE + k)
        return carry

    lax.fori_loop(0, STEPS, drain, 0)
    sent(gr1.at[:, :, pl.ds(H, GH)], G_E1 + 8)
    sent(gr2, G_Y)
    sent(gr3, G_E0)

    @pl.when(jnp.logical_not(stays))
    def _():
        for h in range(2):
            sent(x_own.at[halves[h]], I_PERM + h)

    @pl.when(jnp.logical_and(moved, turn))
    def _():
        for h in range(2):
            sent(x_own.at[halves[h]], I_WAY + h)

    for i in range(2):
        sent(half_rows(z, 0, 0), I_YL + i)
    for i in range(8):
        sent(half_rows(z, 0, 0), I_Z1 + i)
    for i in range(4):
        sent(half_rows(z, 0, 0), I_Z2 + i)
    for i in range(2):
        sent(xz1.at[i], X_Z1 + i)
    for i in range(3):
        sent(sel.at[0], S_ALL + i)
    for i in range(4):
        sent(place(z, c, 0, 2), I_CORE + i)
        sent(xz2.at[0, 0], X_Z2 + i)
    sent(xyl, X_YL)
    for s in range(7):
        sent(tsend.at[s], T_ALL + s)


def copy_kernel(n, *refs):
    held, into, out = refs[2 * n:3 * n], refs[3 * n], refs[3 * n + 1]
    parts = [(i, slice(None)) for i in range(1, n)]
    parts += [(0, pl.ds(r, 64)) for r in range(0, 512, 64)]
    first = [pltpu.make_async_copy(refs[i].at[r], held[i].at[r], into.at[p]) for p, (i, r) in enumerate(parts)]
    second = [pltpu.make_async_copy(held[i].at[r], refs[n + i].at[r], out.at[p]) for p, (i, r) in enumerate(parts)]
    for copy in first:
        copy.start()
    for one, two in zip(first, second):
        one.wait()
        two.start()
    for copy in second:
        copy.wait()


def copy_out(*arrays):
    hbm = pl.BlockSpec(memory_space=pl.ANY)
    n = len(arrays)
    return pl.pallas_call(
        functools.partial(copy_kernel, n),
        out_shape=tuple(jax.ShapeDtypeStruct(a.shape, a.dtype) for a in arrays),
        in_specs=[hbm] * n,
        out_specs=(hbm,) * n,
        scratch_shapes=[pltpu.VMEM(a.shape, a.dtype) for a in arrays]
        + [pltpu.SemaphoreType.DMA((n + 7,)), pltpu.SemaphoreType.DMA((n + 7,))],
    )(*arrays)


def main_grad_wide(
    x_quant, x_scale, user_feats, scenario_ids, scenario_table, label_mask, saved_z, out_grad, gate_a, gate_b,
):
    onehot = (scenario_ids[:, None] == jnp.arange(32, dtype=jnp.int32)[None, :]).astype(BF16)
    scen_rows = jnp.dot(onehot, scenario_table, preferred_element_type=F32).astype(BF16)
    gate_in = jnp.concatenate([user_feats, scen_rows], axis=1)
    a_act = jnp.maximum(jnp.dot(gate_in, gate_a[0], preferred_element_type=F32), 0.0).astype(BF16)
    gate = 2.0 * jax.nn.sigmoid(jnp.dot(a_act, gate_b[0], preferred_element_type=F32))
    masked = out_grad[0].astype(F32) * label_mask.astype(F32)
    z_grad = (masked * gate * (saved_z[0] > 0)).astype(BF16)
    blocks = x_scale.shape[1]
    own = (
        x_quant.astype(F32).reshape(ROWS, blocks, -1) * x_scale.astype(F32)[:, :, None]
    ).reshape(ROWS, -1).astype(BF16)
    inputs = lax.all_to_all(jnp.broadcast_to(own, (16, *own.shape)), "task", 0, 0)
    partial = jnp.einsum("trd,rh->tdh", inputs, z_grad, preferred_element_type=F32).astype(BF16)
    parts = lax.all_to_all(partial.reshape(8, 512, H), "batch", 0, 0)
    return jnp.sum(parts.astype(F32), axis=0).astype(BF16)


def body(
    x_quant, x_scale, user_feats, scenario_ids, scenario_table, label_mask,
    saved_z, out_grad, main_weight, gate_a, gate_b,
):
    vmem = pl.BlockSpec(memory_space=pltpu.VMEM)
    hbm = pl.BlockSpec(memory_space=pl.ANY)
    outs = pl.pallas_call(
        kernel,
        out_shape=(
            jax.ShapeDtypeStruct((512, H), BF16),
            jax.ShapeDtypeStruct((64, GH), BF16),
            jax.ShapeDtypeStruct((64, H), BF16),
            jax.ShapeDtypeStruct((ROWS, 256), BF16),
            jax.ShapeDtypeStruct((USER, ROWS), BF16),
            jax.ShapeDtypeStruct((32, 128), F32),
            jax.ShapeDtypeStruct((1, 1), F32),
        ),
        in_specs=[vmem] * 4 + [hbm] * 7,
        out_specs=(hbm,) + (vmem,) * 5 + (pl.BlockSpec(memory_space=pltpu.SMEM),),
        scratch_shapes=[
            pltpu.VMEM((ROWS, 256), BF16),
            pltpu.VMEM((ROWS, UD), BF16),
            pltpu.VMEM((GH, GH), BF16),
            pltpu.VMEM((GH, H), BF16),
            pltpu.VMEM((ROWS, H), BF16),
            pltpu.VMEM((ROWS, H), BF16),
            pltpu.VMEM((2, 512, H), BF16),
            pltpu.VMEM((ROWS, H), BF16),
            pltpu.VMEM((DEPTH, H), BF16),
            pltpu.VMEM((ROWS, GH), BF16),
            pltpu.VMEM((2, ROWS, GH), BF16),
            pltpu.VMEM((ROWS, GH), F32),
            pltpu.VMEM((512, ROWS), F32),
            pltpu.VMEM((2, 2, 256, 4 * ROWS), BF16),
            pltpu.VMEM((2, 2, 256, DEPTH), BF16),
            pltpu.VMEM((256, ROWS), BF16),
            pltpu.VMEM((256, ROWS), BF16),
            pltpu.VMEM((CAP, ROWS), BF16),
            pltpu.VMEM((4, 8, ROWS), F32),
            pltpu.VMEM((2, 2, 128, H + GH), BF16),
            pltpu.VMEM((2, 128, H + GH), BF16),
            pltpu.VMEM((128, H + GH), BF16),
            pltpu.VMEM((64, H + GH), BF16),
            pltpu.VMEM((8, XB, ROWS), BF16),
            pltpu.VMEM((8, XB, ROWS), BF16),
            pltpu.VMEM((8, XB, ROWS), BF16),
            pltpu.VMEM((2, XB, ROWS), BF16),
            pltpu.VMEM((2, 2, XB, ROWS), BF16),
            pltpu.VMEM((XB, ROWS), BF16),
            pltpu.VMEM((XB, ROWS), BF16),
            pltpu.VMEM((512, H), BF16),
            pltpu.VMEM((512, H), BF16),
            pltpu.VMEM((512, H), BF16),
            pltpu.VMEM((7, 40, 128), F32),
            pltpu.VMEM((7, 40, 128), F32),
            pltpu.SemaphoreType.DMA((9 + STEPS,)),
            pltpu.SemaphoreType.DMA((N_SEM,)),
            pltpu.SemaphoreType.DMA((N_SEM,)),
        ],
        compiler_params=pltpu.CompilerParams(
            collective_id=0, has_side_effects=True, vmem_limit_bytes=60 * 1024 * 1024),
        cost_estimate=pl.CostEstimate(flops=21_000_000_000, bytes_accessed=28_000_000, transcendentals=1_000_000),
    )(
        x_scale.T, scenario_ids[None, :], scenario_table, label_mask.T, x_quant, user_feats, gate_a[0], gate_b[0],
        saved_z[0], out_grad[0], main_weight[0],
    )
    main, grad_a, grad_b, x_grad, user, table_grad = copy_out(*outs[:6])
    args = (
        x_quant, x_scale, user_feats, scenario_ids, scenario_table, label_mask, saved_z, out_grad, gate_a, gate_b)
    _, main = lax.while_loop(
        lambda carry: carry[0] > 0,
        lambda carry: (jnp.zeros_like(carry[0]), main_grad_wide(*args)),
        (outs[6][0, 0], main))
    return main[None], grad_a[None], grad_b[None], x_grad, user.T, table_grad


def solution(mesh):
    placed = (
        P("batch", "task"),
        P("batch", "task"),
        P("batch", None),
        P("batch"),
        P(),
        P("batch", "task"),
        P("task", "batch", None),
        P("task", "batch", None),
        P("task", None, None),
        P("task", None, None),
        P("task", None, None),
    )
    return jax.shard_map(
        body,
        mesh=mesh,
        in_specs=placed,
        out_specs=(
            P("task", "batch", None),
            P("task", "batch", None),
            P("task", "batch", None),
            P("batch", "task"),
            P("batch", "task"),
            P(),
        ),
        check_vma=False,
    )
```

```python
import functools

import jax
import jax.numpy as jnp
from jax import lax
from jax.experimental import pallas as pl
from jax.experimental.pallas import tpu as pltpu
from jax.sharding import PartitionSpec as P

MESH = pl.DeviceIdType.MESH
F32 = jnp.float32
BF16 = jnp.bfloat16

ROWS = 512
H = 2048
GH = 512
UD = 384
CH = 256
STEPS = H // CH
XB = 288
USER = 24
CAP = 320
DEPTH = 4 * CAP
FIRST = 4
AHEAD = 2
LAG = 2

Z_Y, Z_E0, Z_FW = 0, 8, 16
G_E1, G_Y, G_E0 = 24, 33, 34
I_PERM, I_YL, I_Z1, I_Z2, I_CORE = 35, 37, 39, 47, 51
M_E1 = 55
X_CORE, X_Z1, X_Z2, X_YL = 63, 71, 73, 77
T_ALL = 78
S_ALL = 85
I_WAY = 88
N_SEM = 90


def nt(a, b):
    return lax.dot_general(a, b, (((1,), (1,)), ((), ())), preferred_element_type=F32)


def nn(a, b):
    return jnp.dot(a, b, preferred_element_type=F32)


def kernel(
    xs, ids, table, mask_in, xq_hbm, feats_hbm, ga_hbm, gb_hbm, sz_hbm, og_hbm, w_hbm,
    main_out, ga_out, gb_out, x_out, user_out, table_out, flag_out,
    xq, feats, ga, gb, sz, og, wbuf, zfull, zc, gin_in, act, a_back, gint, aall, ac, x_own, x_way, pick, sel,
    gpart, gr1, gr2, gr3, xsend, xkeep, xcore, xz1, xz2, xylsend, xyl, ps, pr, main_v, tsend, trecv,
    lsem, ssem, rsem,
):
    bi = lax.axis_index("batch")
    ti = lax.axis_index("task")
    yh, x = bi // 4, bi % 4
    yl, z, c = ti // 8, (ti // 2) % 4, ti % 2
    x0 = x + 1 - 2 * (x % 2)
    x1 = 3 - x
    xp = x // 2
    z0 = z + 1 - 2 * (z % 2)

    def dev(yh_, x_, yl_, z_, c_):
        return (yh_ * 4 + x_, yl_ * 8 + z_ * 2 + c_)

    d_y = dev(1 - yh, x, yl, z, c)
    d_e0 = dev(yh, x0, yl, z, c)
    d_e1 = dev(yh, x1, yl, z, c)
    d_c = dev(yh, x, yl, z, 1 - c)
    d_yl = dev(yh, x, 1 - yl, z, c)
    d_zp = dev(yh, x, yl, (z + 1) % 4, c)
    d_zm = dev(yh, x, yl, (z + 3) % 4, c)
    member = jnp.logical_or(z == x, z == 3 - x)
    moved = jnp.logical_not(member)
    turn = yh != yl
    d_diag = dev(1 - yh, x0, yl, z, c)
    d_xz = dev(yh, x0, yl, z0, c)
    d_turn = dev(yl, x, yh, z, c)

    def rcopy(src, dst, i, target):
        return pltpu.make_async_remote_copy(
            src_ref=src, dst_ref=dst, send_sem=ssem.at[i], recv_sem=rsem.at[i],
            device_id=target, device_id_type=MESH)

    def send(src, dst, i, target):
        rcopy(src, dst, i, target).start()

    def got(ref, i):
        rcopy(ref, ref, i, d_c).wait_recv()

    def sent(ref, i):
        rcopy(ref, ref, i, d_c).wait_send()

    def packed(s):
        return pl.ds(pl.multiple_of(s * CAP, CAP), CAP)

    def cols(k):
        return pl.ds(pl.multiple_of(k * CH, CH), CH)

    def wcopy(k):
        return pltpu.make_async_copy(
            w_hbm.at[pl.ds(pl.multiple_of(k * 512, 512), 512)], wbuf.at[k % 2], lsem.at[2 + k % 2])

    loads = [
        pltpu.make_async_copy(src, dst, lsem.at[i]) for i, src, dst in (
            (5, xq_hbm, xq), (6, feats_hbm, feats), (7, ga_hbm, ga), (8, gb_hbm, gb), (0, sz_hbm, sz), (1, og_hbm, og))
    ]
    for load in loads:
        load.start()
    wcopy(0).start()
    wcopy(1).start()

    barrier = pltpu.get_barrier_semaphore()
    for target in (d_y, d_e0, d_e1, d_c, d_yl, d_zp, d_zm, d_diag):
        pl.semaphore_signal(barrier, inc=1, device_id=target, device_id_type=MESH)

    @pl.when(moved)
    def _():
        pl.semaphore_signal(barrier, inc=1, device_id=d_xz, device_id_type=MESH)

    @pl.when(turn)
    def _():
        pl.semaphore_signal(barrier, inc=1, device_id=d_turn, device_id_type=MESH)

    loads[0].wait()
    half = xq.shape[1] // 2
    for j in range(2):
        part = xq[:, j * half:(j + 1) * half].astype(F32).T * xs[j:j + 1, :].astype(F32)
        x_own[j * half:(j + 1) * half, :] = part.astype(BF16)

    mask_row = jnp.broadcast_to(mask_in[...], (8, ROWS)).astype(F32)
    before = (
        lax.broadcasted_iota(jnp.int32, (ROWS, ROWS), 0) < lax.broadcasted_iota(jnp.int32, (ROWS, ROWS), 1)
    ).astype(BF16)
    rank = nn(mask_row.astype(BF16), before)
    sel[yh] = jnp.where(mask_row > 0, rank, -1.0)

    def picker(s):
        return (
            lax.broadcasted_iota(jnp.int32, (CAP, ROWS), 0).astype(F32) == sel[s, 0:1, :]
        ).astype(BF16)

    pick[...] = picker(yh)

    pl.semaphore_wait(barrier, 8 + jnp.where(moved, 1, 0) + jnp.where(turn, 1, 0))

    def place(zz, core, first, count):
        d_ = jnp.where(zz // 2 == xp, 1, 0)
        k_ = jnp.where(jnp.logical_or(zz == x, zz == 3 - x), 0, 1)
        off = pl.multiple_of((k_ * 2 + first) * ROWS, ROWS)
        return aall.at[d_, core, :, pl.ds(off, count * ROWS)]

    def half_rows(zz, first, h):
        d_ = jnp.where(zz // 2 == xp, 1, 0)
        k_ = jnp.where(jnp.logical_or(zz == x, zz == 3 - x), 0, 1)
        off = pl.multiple_of((k_ * 2 + first) * ROWS, ROWS)
        return aall.at[d_, c, pl.ds(h * 128, 128), pl.ds(off, ROWS)]

    halves = [pl.ds(h * 128, 128) for h in range(2)]
    stays = jnp.logical_and(member, jnp.logical_not(turn))

    @pl.when(stays)
    def _():
        local = pltpu.make_async_copy(x_own, place(z, c, yl, 1), lsem.at[4])
        local.start()
        local.wait()

    @pl.when(jnp.logical_and(member, turn))
    def _():
        for h in range(2):
            send(x_own.at[halves[h]], half_rows(z, yh, h), I_PERM + h, d_turn)

    @pl.when(jnp.logical_and(moved, jnp.logical_not(turn)))
    def _():
        for h in range(2):
            send(x_own.at[halves[h]], half_rows(z, yl, h), I_PERM + h, d_xz)

    @pl.when(jnp.logical_and(moved, turn))
    def _():
        for h in range(2):
            send(x_own.at[halves[h]], x_way.at[halves[h]], I_WAY + h, d_xz)

    def turn_way(h):
        @pl.when(jnp.logical_and(moved, turn))
        def _():
            got(x_way.at[halves[h]], I_WAY + h)
            send(x_way.at[halves[h]], half_rows(z, yh, h), I_PERM + h, d_turn)

    send(sel.at[yh], sel.at[yh], S_ALL, d_y)
    send(sel.at[yh], sel.at[2 + yh], S_ALL + 1, d_e0)
    send(sel.at[yh], sel.at[2 + yh], S_ALL + 2, d_diag)

    onehot_t = (ids[...] == lax.broadcasted_iota(jnp.int32, (32, ROWS), 0)).astype(F32)
    for load in loads[1:]:
        load.wait()
    gin_in[:, :UD] = feats[...]
    gin_in[:, UD:] = nn(onehot_t.T.astype(BF16), table[...]).astype(BF16)
    a_pre = nn(gin_in[...], ga[...])
    a_act = jnp.maximum(a_pre, 0.0)
    act[0] = a_act.astype(BF16)
    act[1] = a_act.T.astype(BF16)
    a_back[...] = jnp.zeros_like(a_back)
    mask = mask_row.T[:, 0:1]

    def send_e0(n):
        send(zc.at[packed(yh), cols(n)], zc.at[packed(2 + yh), cols(n)], Z_E0 + n, d_e0)

    relay = jnp.logical_and(moved, turn)

    def arrived(h):
        mine = half_rows(z, yl, h)

        @pl.when(jnp.logical_not(stays))
        def _():
            got(mine, I_PERM + h)

        send(mine, mine, I_YL + h, d_yl)
        send(mine, mine, I_Z1 + 2 * h, d_zp)
        send(mine, mine, I_Z1 + 2 * h + 1, d_zm)

    def first(k, carry):
        cc = pl.ds(pl.multiple_of(k * 2 * CH, 2 * CH), 2 * CH)
        gate = 2.0 * jax.nn.sigmoid(nn(act[0], gb[:, cc]))
        masked = og[:, cc].astype(F32) * mask
        pre = sz[:, cc].astype(F32)
        mg = masked * gate
        zk = jnp.where(pre > 0, mg, 0.0).astype(BF16)
        zfull[:, cc] = zk
        zc[packed(yh), cc] = nn(pick[...], zk).astype(BF16)
        u = (jnp.maximum(pre, 0.0) * mg * (1.0 - 0.5 * gate)).astype(BF16)
        part = nn(act[1], u).astype(BF16)
        for i in range(2):
            for j in range(2):
                r = (i * 2 + j) * 128
                gpart[i, j, :, cc] = part[r:r + 128]
        a_back[...] += nt(u, gb[:, cc])

        @pl.when(k < FIRST // 2)
        def _():
            send_e0(2 * k)
            send_e0(2 * k + 1)

        for h in range(2):
            one = cols(2 * k + h)
            send(gpart.at[:, 1 - xp, :, one], gr1.at[:, :, one], G_E1 + 2 * k + h, d_e1)

        for h in range(2):

            @pl.when(k == h)
            def _():
                turn_way(h)

            @pl.when(k == jnp.where(relay, h + 2, h + 1))
            def _():
                arrived(h)

        return carry

    lax.fori_loop(0, STEPS // 2, first, 0)

    zn, zb, zf = (z + 1) % 4, (z + 3) % 4, (z + 2) % 4

    def z_low(n, first):
        low = half_rows(zb, first, 0)
        got(low, I_Z1 + 4 * n)
        send(low, low, I_Z2 + 2 * n, d_zp)

    def z_high(n, first):
        high = half_rows(zn, first, 1)
        got(high, I_Z1 + 4 * n + 3)
        send(high, high, I_Z2 + 2 * n + 1, d_zm)

    def z_rest(n, first):
        got(half_rows(zn, first, 0), I_Z1 + 4 * n + 1)
        got(half_rows(zb, first, 1), I_Z1 + 4 * n + 2)

    def to_core(zz, i):
        mine = place(zz, c, 0, 2)
        send(mine, mine, I_CORE + i, d_c)

    def from_y(h):
        near = half_rows(z, 1 - yl, h)
        got(near, I_YL + h)
        send(near, near, I_Z1 + 4 + 2 * h, d_zp)
        send(near, near, I_Z1 + 4 + 2 * h + 1, d_zm)

    def send_y(n, carry):
        send(zc.at[packed(yh), cols(n)], zc.at[packed(yh), cols(n)], Z_Y + n, d_y)
        return carry

    from_y(0)
    lax.fori_loop(0, 2, send_y, 0)
    z_low(0, yl)

    a_grad = jnp.where(act[0].astype(F32) > 0, a_back[...], 0.0).astype(BF16)
    part = nn(gin_in[...].astype(F32).T.astype(BF16), a_grad).astype(BF16)
    for i in range(2):
        for j in range(2):
            r = (i * 2 + j) * 128
            gpart[i, j, :, H:] = part[r:r + 128]
    send(gpart.at[:, 1 - xp, :, pl.ds(H, GH)], gr1.at[:, :, pl.ds(H, GH)], G_E1 + 8, d_e1)
    gint[...] = nt(ga[...], a_grad)
    scen = nt(a_grad, ga[UD:, :])
    tsend[0, :32] = lax.dot_general(
        onehot_t, scen, (((1,), (0,)), ((), ())), precision=lax.Precision.HIGHEST, preferred_element_type=F32)
    over = jnp.maximum(jnp.sum(mask_row, axis=1, keepdims=True) - CAP, 0.0)
    tsend[0, 32:] = jnp.broadcast_to(over, (8, 128))
    t_partners = (d_c, dev(yh, x, yl, z0, c), dev(yh, x, yl, 3 - z, c), d_e1, d_e0, d_yl, d_y)
    send(tsend.at[0], trecv.at[0], T_ALL, t_partners[0])

    def user_rows(t):
        rows = gint[pl.ds(pl.multiple_of(t * USER, 8), USER), :]
        return jnp.concatenate([rows, jnp.zeros((XB - 256 - USER, ROWS), F32)], axis=0).astype(BF16)

    from_y(1)

    lax.fori_loop(2, STEPS, send_y, 0)
    to_core(z, 0)
    z_high(0, yl)

    def x_block(k, carry):
        wcopy(k).wait()
        wrows = wbuf.at[k % 2]
        other = 1 - c
        xsend[k, :256, :] = nt(wrows[pl.ds(pl.multiple_of(other * 256, 256), 256), :], zfull[...]).astype(BF16)
        xsend[k, 256:, :] = user_rows(k * 2 + other)
        send(xsend.at[k], xcore.at[k], X_CORE + k, d_c)
        xkeep[k, :256, :] = nt(wrows[pl.ds(pl.multiple_of(c * 256, 256), 256), :], zfull[...]).astype(BF16)
        xkeep[k, 256:, :] = user_rows(k * 2 + c)

        @pl.when(k < STEPS - 2)
        def _():
            wcopy(k + 2).start()

        return carry

    def inputs_z2():
        for n, first in enumerate((yl, 1 - yl)):
            got(half_rows(zf, first, 0), I_Z2 + 2 * n)
            got(half_rows(zf, first, 1), I_Z2 + 2 * n + 1)
        to_core(zf, 3)

    def forward(k):
        cc = cols(k)
        got(zc.at[packed(1 - yh), cc], Z_Y + k)
        send(zc.at[packed(1 - yh), cc], zc.at[packed(3 - yh), cc], Z_FW + k, d_e0)

        @pl.when(jnp.logical_and(k >= 2, k < 6))
        def _():
            send_e0(k + 2)

    def table_step(s):
        got(trecv.at[s - 1], T_ALL + s - 1)
        tsend[s] = tsend[s - 1] + trecv[s - 1]
        send(tsend.at[s], trecv.at[s], T_ALL + s, t_partners[s])

    def wait_inputs():
        for i, zz in enumerate((z, zb, zn, zf)):
            got(place(zz, 1 - c, 0, 2), I_CORE + i)
        got(sel.at[1 - yh], S_ALL)
        got(sel.at[2 + yh], S_ALL + 1)
        got(sel.at[3 - yh], S_ALL + 2)

    def pack_inputs(d_):
        for s in range(4):
            p = picker(s)
            for j in range(2):
                ac[d_, j, :, s * CAP:(s + 1) * CAP] = nt(
                    aall[d_, j, :, s * ROWS:(s + 1) * ROWS], p).astype(BF16)

    def core_sum():
        def one(n, carry):
            got(xcore.at[n], X_CORE + n)
            xkeep[n] = (xkeep[n].astype(F32) + xcore[n].astype(F32)).astype(BF16)
            return carry

        lax.fori_loop(0, STEPS, one, 0)
        send(xkeep.at[zf], xz1.at[0], X_Z1, d_zp)
        send(xkeep.at[4 + zf], xz1.at[1], X_Z1 + 1, d_zm)

    def gate_e1():
        for n in range(STEPS):
            got(gr1.at[:, :, pl.ds(n * CH, CH)], G_E1 + n)
        got(gr1.at[:, :, pl.ds(H, GH)], G_E1 + 8)
        gpart[1 - yh, xp] = (gpart[1 - yh, xp].astype(F32) + gr1[1 - yh].astype(F32)).astype(BF16)
        send(gpart.at[1 - yh, xp], gr2, G_Y, d_y)

    def gate_y():
        got(gr2, G_Y)
        gpart[yh, xp] = (
            gpart[yh, xp].astype(F32) + gr1[yh].astype(F32) + gr2[...].astype(F32)).astype(BF16)
        far = pl.ds(pl.multiple_of((x0 % 2) * 64, 64), 64)
        send(gpart.at[yh, xp, far], gr3, G_E0, d_e0)

    def gate_e0():
        got(gr3, G_E0)
        near = pl.ds(pl.multiple_of((x % 2) * 64, 64), 64)
        total = gpart[yh, xp, near, :].astype(F32) + gr3[...].astype(F32)
        gb_out[...] = total[:, :H].astype(BF16)
        ga_out[...] = total[:, H:].astype(BF16)

    def x_z1():
        got(xz1.at[0], X_Z1)
        got(xz1.at[1], X_Z1 + 1)
        xkeep[zn] = (xkeep[zn].astype(F32) + xz1[0].astype(F32)).astype(BF16)
        xkeep[4 + zb] = (xkeep[4 + zb].astype(F32) + xz1[1].astype(F32)).astype(BF16)
        for h in range(2):
            send(xkeep.at[h * 4 + zn], xz2.at[0, h], X_Z2 + 2 * h, d_zp)
            send(xkeep.at[h * 4 + zb], xz2.at[1, h], X_Z2 + 1 + 2 * h, d_zm)

    def x_z2():
        for h in range(2):
            got(xz2.at[0, h], X_Z2 + 2 * h)
            got(xz2.at[1, h], X_Z2 + 1 + 2 * h)
        xylsend[...] = (
            xkeep[(1 - yl) * 4 + z].astype(F32) + xz2[0, 1 - yl].astype(F32) + xz2[1, 1 - yl].astype(F32)
        ).astype(BF16)
        send(xylsend, xyl, X_YL, d_yl)

    def x_last():
        got(xyl, X_YL)
        total = (
            xkeep[yl * 4 + z].astype(F32) + xz2[0, yl].astype(F32) + xz2[1, yl].astype(F32)
            + xyl[...].astype(F32))
        x_out[...] = total[:256].T.astype(BF16)
        user_out[...] = total[256:256 + USER].astype(BF16)

    def table_last():
        got(trecv.at[6], T_ALL + 6)
        total = tsend[6] + trecv[6]
        table_out[...] = total[:32]
        flag_out[0, 0] = total[32, 0]

    def table_at(s):
        return lambda: table_step(s)

    extra = {
        1: (table_at(1),),
        2: (table_at(2),),
        3: (table_at(3),),
        4: (core_sum, lambda: pack_inputs(1)),
        5: (gate_e1,),
        6: (x_z1, table_at(4)),
        8: (table_at(5),),
        9: (x_z2, gate_y, table_at(6)),
        11: (x_last, gate_e0, table_last),
    }

    def main_copy(n):
        return pltpu.make_async_copy(main_v.at[:, cols(n)], main_out.at[:, cols(n)], lsem.at[9 + n])

    def step(i, carry):
        j = i - LAG

        @pl.when(i == 1)
        def _():
            def x_and_forward(n, carry):
                x_block(n + 2, carry)
                forward(n)
                return carry

            lax.fori_loop(0, 2, x_and_forward, 0)
            inputs_z2()
            forward(2)

        @pl.when(i == LAG)
        def _():
            wait_inputs()
            pack_inputs(0)

        @pl.when(jnp.logical_and(j >= 0, j < STEPS))
        def _():
            cc = cols(j)
            got(zc.at[packed(2 + yh), cc], Z_E0 + j)
            got(zc.at[packed(3 - yh), cc], Z_FW + j)
            for h in range(2):
                ps[h * 256:(h + 1) * 256, cc] = nn(ac[0, h], zc[:, cc]).astype(BF16)
            send(ps.at[:, cc], pr.at[:, cc], M_E1 + j, d_e1)

        @pl.when(jnp.logical_and(i >= 2, i < 5))
        def _():
            @pl.when(i > 2)
            def _():
                forward(2 * i - 2)

            forward(2 * i - 1)

        @pl.when(jnp.logical_and(i < 4, i != 1))
        def _():
            lax.fori_loop(2 * i, 2 * i + 2, x_block, 0)

        @pl.when(i == 0)
        def _():
            z_low(1, 1 - yl)
            z_high(1, 1 - yl)
            for n, first in enumerate((yl, 1 - yl)):
                z_rest(n, first)
            to_core(zb, 1)
            to_core(zn, 2)

        for at, calls in extra.items():

            @pl.when(i == at)
            def _():
                for call in calls:
                    call()

        @pl.when(j >= AHEAD)
        def _():
            cc = cols(j - AHEAD)
            got(pr.at[:, cc], M_E1 + j - AHEAD)
            for h in range(2):
                total = pr[h * 256:(h + 1) * 256, cc].astype(F32) + nn(ac[1, h], zc[:, cc])
                main_v[h * 256:(h + 1) * 256, cc] = total.astype(BF16)
            main_copy(j - AHEAD).start()

        return carry

    lax.fori_loop(0, STEPS + LAG + AHEAD, step, 0)

    def drain(k, carry):
        cc = cols(k)
        main_copy(k).wait()
        sent(zc.at[packed(0), cc], Z_Y + k)
        sent(zc.at[packed(0), cc], Z_E0 + k)
        sent(zc.at[packed(0), cc], Z_FW + k)
        sent(gr1.at[:, :, cc], G_E1 + k)
        sent(ps.at[:, cc], M_E1 + k)
        sent(xsend.at[k], X_CORE + k)
        return carry

    lax.fori_loop(0, STEPS, drain, 0)
    sent(gr1.at[:, :, pl.ds(H, GH)], G_E1 + 8)
    sent(gr2, G_Y)
    sent(gr3, G_E0)

    @pl.when(jnp.logical_not(stays))
    def _():
        for h in range(2):
            sent(x_own.at[halves[h]], I_PERM + h)

    @pl.when(jnp.logical_and(moved, turn))
    def _():
        for h in range(2):
            sent(x_own.at[halves[h]], I_WAY + h)

    for i in range(2):
        sent(half_rows(z, 0, 0), I_YL + i)
    for i in range(8):
        sent(half_rows(z, 0, 0), I_Z1 + i)
    for i in range(4):
        sent(half_rows(z, 0, 0), I_Z2 + i)
    for i in range(2):
        sent(xz1.at[i], X_Z1 + i)
    for i in range(3):
        sent(sel.at[0], S_ALL + i)
    for i in range(4):
        sent(place(z, c, 0, 2), I_CORE + i)
        sent(xz2.at[0, 0], X_Z2 + i)
    sent(xyl, X_YL)
    for s in range(7):
        sent(tsend.at[s], T_ALL + s)


def copy_kernel(n, *refs):
    held, into, out = refs[2 * n:3 * n], refs[3 * n], refs[3 * n + 1]
    parts = [(i, slice(None)) for i in range(1, n)]
    parts += [(0, pl.ds(r, 64)) for r in range(0, 512, 64)]
    first = [pltpu.make_async_copy(refs[i].at[r], held[i].at[r], into.at[p]) for p, (i, r) in enumerate(parts)]
    second = [pltpu.make_async_copy(held[i].at[r], refs[n + i].at[r], out.at[p]) for p, (i, r) in enumerate(parts)]
    for copy in first:
        copy.start()
    for one, two in zip(first, second):
        one.wait()
        two.start()
    for copy in second:
        copy.wait()


def copy_out(*arrays):
    hbm = pl.BlockSpec(memory_space=pl.ANY)
    n = len(arrays)
    return pl.pallas_call(
        functools.partial(copy_kernel, n),
        out_shape=tuple(jax.ShapeDtypeStruct(a.shape, a.dtype) for a in arrays),
        in_specs=[hbm] * n,
        out_specs=(hbm,) * n,
        scratch_shapes=[pltpu.VMEM(a.shape, a.dtype) for a in arrays]
        + [pltpu.SemaphoreType.DMA((n + 7,)), pltpu.SemaphoreType.DMA((n + 7,))],
    )(*arrays)


def main_grad_wide(
    x_quant, x_scale, user_feats, scenario_ids, scenario_table, label_mask, saved_z, out_grad, gate_a, gate_b,
):
    onehot = (scenario_ids[:, None] == jnp.arange(32, dtype=jnp.int32)[None, :]).astype(BF16)
    scen_rows = jnp.dot(onehot, scenario_table, preferred_element_type=F32).astype(BF16)
    gate_in = jnp.concatenate([user_feats, scen_rows], axis=1)
    a_act = jnp.maximum(jnp.dot(gate_in, gate_a[0], preferred_element_type=F32), 0.0).astype(BF16)
    gate = 2.0 * jax.nn.sigmoid(jnp.dot(a_act, gate_b[0], preferred_element_type=F32))
    masked = out_grad[0].astype(F32) * label_mask.astype(F32)
    z_grad = (masked * gate * (saved_z[0] > 0)).astype(BF16)
    blocks = x_scale.shape[1]
    own = (
        x_quant.astype(F32).reshape(ROWS, blocks, -1) * x_scale.astype(F32)[:, :, None]
    ).reshape(ROWS, -1).astype(BF16)
    inputs = lax.all_to_all(jnp.broadcast_to(own, (16, *own.shape)), "task", 0, 0)
    partial = jnp.einsum("trd,rh->tdh", inputs, z_grad, preferred_element_type=F32).astype(BF16)
    parts = lax.all_to_all(partial.reshape(8, 512, H), "batch", 0, 0)
    return jnp.sum(parts.astype(F32), axis=0).astype(BF16)


def body(
    x_quant, x_scale, user_feats, scenario_ids, scenario_table, label_mask,
    saved_z, out_grad, main_weight, gate_a, gate_b,
):
    vmem = pl.BlockSpec(memory_space=pltpu.VMEM)
    hbm = pl.BlockSpec(memory_space=pl.ANY)
    outs = pl.pallas_call(
        kernel,
        out_shape=(
            jax.ShapeDtypeStruct((512, H), BF16),
            jax.ShapeDtypeStruct((64, GH), BF16),
            jax.ShapeDtypeStruct((64, H), BF16),
            jax.ShapeDtypeStruct((ROWS, 256), BF16),
            jax.ShapeDtypeStruct((USER, ROWS), BF16),
            jax.ShapeDtypeStruct((32, 128), F32),
            jax.ShapeDtypeStruct((1, 1), F32),
        ),
        in_specs=[vmem] * 4 + [hbm] * 7,
        out_specs=(hbm,) + (vmem,) * 5 + (pl.BlockSpec(memory_space=pltpu.SMEM),),
        scratch_shapes=[
            pltpu.VMEM((ROWS, 256), BF16),
            pltpu.VMEM((ROWS, UD), BF16),
            pltpu.VMEM((GH, GH), BF16),
            pltpu.VMEM((GH, H), BF16),
            pltpu.VMEM((ROWS, H), BF16),
            pltpu.VMEM((ROWS, H), BF16),
            pltpu.VMEM((2, 512, H), BF16),
            pltpu.VMEM((ROWS, H), BF16),
            pltpu.VMEM((DEPTH, H), BF16),
            pltpu.VMEM((ROWS, GH), BF16),
            pltpu.VMEM((2, ROWS, GH), BF16),
            pltpu.VMEM((ROWS, GH), F32),
            pltpu.VMEM((512, ROWS), F32),
            pltpu.VMEM((2, 2, 256, 4 * ROWS), BF16),
            pltpu.VMEM((2, 2, 256, DEPTH), BF16),
            pltpu.VMEM((256, ROWS), BF16),
            pltpu.VMEM((256, ROWS), BF16),
            pltpu.VMEM((CAP, ROWS), BF16),
            pltpu.VMEM((4, 8, ROWS), F32),
            pltpu.VMEM((2, 2, 128, H + GH), BF16),
            pltpu.VMEM((2, 128, H + GH), BF16),
            pltpu.VMEM((128, H + GH), BF16),
            pltpu.VMEM((64, H + GH), BF16),
            pltpu.VMEM((8, XB, ROWS), BF16),
            pltpu.VMEM((8, XB, ROWS), BF16),
            pltpu.VMEM((8, XB, ROWS), BF16),
            pltpu.VMEM((2, XB, ROWS), BF16),
            pltpu.VMEM((2, 2, XB, ROWS), BF16),
            pltpu.VMEM((XB, ROWS), BF16),
            pltpu.VMEM((XB, ROWS), BF16),
            pltpu.VMEM((512, H), BF16),
            pltpu.VMEM((512, H), BF16),
            pltpu.VMEM((512, H), BF16),
            pltpu.VMEM((7, 40, 128), F32),
            pltpu.VMEM((7, 40, 128), F32),
            pltpu.SemaphoreType.DMA((9 + STEPS,)),
            pltpu.SemaphoreType.DMA((N_SEM,)),
            pltpu.SemaphoreType.DMA((N_SEM,)),
        ],
        compiler_params=pltpu.CompilerParams(
            collective_id=0, has_side_effects=True, vmem_limit_bytes=60 * 1024 * 1024),
        cost_estimate=pl.CostEstimate(flops=21_000_000_000, bytes_accessed=28_000_000, transcendentals=1_000_000),
    )(
        x_scale.T, scenario_ids[None, :], scenario_table, label_mask.T, x_quant, user_feats, gate_a[0], gate_b[0],
        saved_z[0], out_grad[0], main_weight[0],
    )
    main, grad_a, grad_b, x_grad, user, table_grad = copy_out(*outs[:6])
    args = (
        x_quant, x_scale, user_feats, scenario_ids, scenario_table, label_mask, saved_z, out_grad, gate_a, gate_b)
    _, main = lax.while_loop(
        lambda carry: carry[0] > 0,
        lambda carry: (jnp.zeros_like(carry[0]), main_grad_wide(*args)),
        (outs[6][0, 0], main))
    return main[None], grad_a[None], grad_b[None], x_grad, user.T, table_grad


def solution(mesh):
    placed = (
        P("batch", "task"),
        P("batch", "task"),
        P("batch", None),
        P("batch"),
        P(),
        P("batch", "task"),
        P("task", "batch", None),
        P("task", "batch", None),
        P("task", None, None),
        P("task", None, None),
        P("task", None, None),
    )
    return jax.shard_map(
        body,
        mesh=mesh,
        in_specs=placed,
        out_specs=(
            P("task", "batch", None),
            P("task", "batch", None),
            P("task", "batch", None),
            P("batch", "task"),
            P("batch", "task"),
            P(),
        ),
        check_vma=False,
    )
```

```python
import functools

import jax
import jax.numpy as jnp
from jax import lax
from jax.experimental import pallas as pl
from jax.experimental.pallas import tpu as pltpu
from jax.sharding import PartitionSpec as P

MESH = pl.DeviceIdType.MESH
F32 = jnp.float32
BF16 = jnp.bfloat16

ROWS = 512
H = 2048
GH = 512
UD = 384
CH = 256
STEPS = H // CH
XB = 288
USER = 24
CAP = 320
DEPTH = 4 * CAP
FIRST = 4
AHEAD = 2
LAG = 2

Z_Y, Z_E0, Z_FW = 0, 8, 16
G_E1, G_Y, G_E0 = 24, 33, 34
I_PERM, I_YL, I_Z1, I_Z2, I_CORE = 35, 37, 39, 47, 51
M_E1 = 55
X_CORE, X_Z1, X_Z2, X_YL = 63, 71, 73, 77
T_ALL = 78
S_ALL = 85
I_WAY = 88
N_SEM = 90


def nt(a, b):
    return lax.dot_general(a, b, (((1,), (1,)), ((), ())), preferred_element_type=F32)


def nn(a, b):
    return jnp.dot(a, b, preferred_element_type=F32)


def kernel(
    xs, ids, table, mask_in, xq_hbm, feats_hbm, ga_hbm, gb_hbm, sz_hbm, og_hbm, w_hbm,
    main_out, ga_out, gb_out, x_out, user_out, table_out, flag_out,
    xq, feats, ga, gb, sz, og, wbuf, zfull, zc, gin_in, act, a_back, gint, aall, ac, x_own, x_way, pick, sel,
    gpart, gr1, gr2, gr3, xsend, xkeep, xcore, xz1, xz2, xylsend, xyl, ps, pr, main_v, tsend, trecv,
    lsem, ssem, rsem,
):
    bi = lax.axis_index("batch")
    ti = lax.axis_index("task")
    yh, x = bi // 4, bi % 4
    yl, z, c = ti // 8, (ti // 2) % 4, ti % 2
    x0 = x + 1 - 2 * (x % 2)
    x1 = 3 - x
    xp = x // 2
    z0 = z + 1 - 2 * (z % 2)

    def dev(yh_, x_, yl_, z_, c_):
        return (yh_ * 4 + x_, yl_ * 8 + z_ * 2 + c_)

    d_y = dev(1 - yh, x, yl, z, c)
    d_e0 = dev(yh, x0, yl, z, c)
    d_e1 = dev(yh, x1, yl, z, c)
    d_c = dev(yh, x, yl, z, 1 - c)
    d_yl = dev(yh, x, 1 - yl, z, c)
    d_zp = dev(yh, x, yl, (z + 1) % 4, c)
    d_zm = dev(yh, x, yl, (z + 3) % 4, c)
    member = jnp.logical_or(z == x, z == 3 - x)
    moved = jnp.logical_not(member)
    turn = yh != yl
    d_diag = dev(1 - yh, x0, yl, z, c)
    d_xz = dev(yh, x0, yl, z0, c)
    d_turn = dev(yl, x, yh, z, c)

    def rcopy(src, dst, i, target):
        return pltpu.make_async_remote_copy(
            src_ref=src, dst_ref=dst, send_sem=ssem.at[i], recv_sem=rsem.at[i],
            device_id=target, device_id_type=MESH)

    def send(src, dst, i, target):
        rcopy(src, dst, i, target).start()

    def got(ref, i):
        rcopy(ref, ref, i, d_c).wait_recv()

    def sent(ref, i):
        rcopy(ref, ref, i, d_c).wait_send()

    def packed(s):
        return pl.ds(pl.multiple_of(s * CAP, CAP), CAP)

    def cols(k):
        return pl.ds(pl.multiple_of(k * CH, CH), CH)

    def wcopy(k):
        return pltpu.make_async_copy(
            w_hbm.at[pl.ds(pl.multiple_of(k * 512, 512), 512)], wbuf.at[k % 2], lsem.at[2 + k % 2])

    loads = [
        pltpu.make_async_copy(src, dst, lsem.at[i]) for i, src, dst in (
            (5, xq_hbm, xq), (6, feats_hbm, feats), (7, ga_hbm, ga), (8, gb_hbm, gb), (0, sz_hbm, sz), (1, og_hbm, og))
    ]
    for load in loads:
        load.start()
    wcopy(0).start()
    wcopy(1).start()

    barrier = pltpu.get_barrier_semaphore()
    for target in (d_y, d_e0, d_e1, d_c, d_yl, d_zp, d_zm, d_diag):
        pl.semaphore_signal(barrier, inc=1, device_id=target, device_id_type=MESH)

    @pl.when(moved)
    def _():
        pl.semaphore_signal(barrier, inc=1, device_id=d_xz, device_id_type=MESH)

    @pl.when(turn)
    def _():
        pl.semaphore_signal(barrier, inc=1, device_id=d_turn, device_id_type=MESH)

    loads[0].wait()
    half = xq.shape[1] // 2
    for j in range(2):
        part = xq[:, j * half:(j + 1) * half].astype(F32).T * xs[j:j + 1, :].astype(F32)
        x_own[j * half:(j + 1) * half, :] = part.astype(BF16)

    mask_row = jnp.broadcast_to(mask_in[...], (8, ROWS)).astype(F32)
    before = (
        lax.broadcasted_iota(jnp.int32, (ROWS, ROWS), 0) < lax.broadcasted_iota(jnp.int32, (ROWS, ROWS), 1)
    ).astype(BF16)
    rank = nn(mask_row.astype(BF16), before)
    sel[yh] = jnp.where(mask_row > 0, rank, -1.0)

    def picker(s):
        return (
            lax.broadcasted_iota(jnp.int32, (CAP, ROWS), 0).astype(F32) == sel[s, 0:1, :]
        ).astype(BF16)

    pick[...] = picker(yh)

    pl.semaphore_wait(barrier, 8 + jnp.where(moved, 1, 0) + jnp.where(turn, 1, 0))

    def place(zz, core, first, count):
        d_ = jnp.where(zz // 2 == xp, 1, 0)
        k_ = jnp.where(jnp.logical_or(zz == x, zz == 3 - x), 0, 1)
        off = pl.multiple_of((k_ * 2 + first) * ROWS, ROWS)
        return aall.at[d_, core, :, pl.ds(off, count * ROWS)]

    def half_rows(zz, first, h):
        d_ = jnp.where(zz // 2 == xp, 1, 0)
        k_ = jnp.where(jnp.logical_or(zz == x, zz == 3 - x), 0, 1)
        off = pl.multiple_of((k_ * 2 + first) * ROWS, ROWS)
        return aall.at[d_, c, pl.ds(h * 128, 128), pl.ds(off, ROWS)]

    halves = [pl.ds(h * 128, 128) for h in range(2)]
    stays = jnp.logical_and(member, jnp.logical_not(turn))

    @pl.when(stays)
    def _():
        local = pltpu.make_async_copy(x_own, place(z, c, yl, 1), lsem.at[4])
        local.start()
        local.wait()

    @pl.when(jnp.logical_and(member, turn))
    def _():
        for h in range(2):
            send(x_own.at[halves[h]], half_rows(z, yh, h), I_PERM + h, d_turn)

    @pl.when(jnp.logical_and(moved, jnp.logical_not(turn)))
    def _():
        for h in range(2):
            send(x_own.at[halves[h]], half_rows(z, yl, h), I_PERM + h, d_xz)

    @pl.when(jnp.logical_and(moved, turn))
    def _():
        for h in range(2):
            send(x_own.at[halves[h]], x_way.at[halves[h]], I_WAY + h, d_xz)

    def turn_way(h):
        @pl.when(jnp.logical_and(moved, turn))
        def _():
            got(x_way.at[halves[h]], I_WAY + h)
            send(x_way.at[halves[h]], half_rows(z, yh, h), I_PERM + h, d_turn)

    send(sel.at[yh], sel.at[yh], S_ALL, d_y)
    send(sel.at[yh], sel.at[2 + yh], S_ALL + 1, d_e0)
    send(sel.at[yh], sel.at[2 + yh], S_ALL + 2, d_diag)

    onehot_t = (ids[...] == lax.broadcasted_iota(jnp.int32, (32, ROWS), 0)).astype(F32)
    for load in loads[1:]:
        load.wait()
    gin_in[:, :UD] = feats[...]
    gin_in[:, UD:] = nn(onehot_t.T.astype(BF16), table[...]).astype(BF16)
    a_pre = nn(gin_in[...], ga[...])
    a_act = jnp.maximum(a_pre, 0.0)
    act[0] = a_act.astype(BF16)
    act[1] = a_act.T.astype(BF16)
    a_back[...] = jnp.zeros_like(a_back)
    mask = mask_row.T[:, 0:1]

    def send_e0(n):
        send(zc.at[packed(yh), cols(n)], zc.at[packed(2 + yh), cols(n)], Z_E0 + n, d_e0)

    relay = jnp.logical_and(moved, turn)

    def arrived(h):
        mine = half_rows(z, yl, h)

        @pl.when(jnp.logical_not(stays))
        def _():
            got(mine, I_PERM + h)

        send(mine, mine, I_YL + h, d_yl)
        send(mine, mine, I_Z1 + 2 * h, d_zp)
        send(mine, mine, I_Z1 + 2 * h + 1, d_zm)

    def first(k, carry):
        cc = pl.ds(pl.multiple_of(k * 2 * CH, 2 * CH), 2 * CH)
        gate = 2.0 * jax.nn.sigmoid(nn(act[0], gb[:, cc]))
        masked = og[:, cc].astype(F32) * mask
        pre = sz[:, cc].astype(F32)
        mg = masked * gate
        zk = jnp.where(pre > 0, mg, 0.0).astype(BF16)
        zfull[:, cc] = zk
        zc[packed(yh), cc] = nn(pick[...], zk).astype(BF16)
        u = (jnp.maximum(pre, 0.0) * mg * (1.0 - 0.5 * gate)).astype(BF16)
        part = nn(act[1], u).astype(BF16)
        for i in range(2):
            for j in range(2):
                r = (i * 2 + j) * 128
                gpart[i, j, :, cc] = part[r:r + 128]
        a_back[...] += nt(u, gb[:, cc])

        @pl.when(k < FIRST // 2)
        def _():
            send_e0(2 * k)
            send_e0(2 * k + 1)

        for h in range(2):
            one = cols(2 * k + h)
            send(gpart.at[:, 1 - xp, :, one], gr1.at[:, :, one], G_E1 + 2 * k + h, d_e1)

        for h in range(2):

            @pl.when(k == h)
            def _():
                turn_way(h)

            @pl.when(k == jnp.where(relay, h + 2, h + 1))
            def _():
                arrived(h)

        return carry

    lax.fori_loop(0, STEPS // 2, first, 0)

    zn, zb, zf = (z + 1) % 4, (z + 3) % 4, (z + 2) % 4

    def z_low(n, first):
        low = half_rows(zb, first, 0)
        got(low, I_Z1 + 4 * n)
        send(low, low, I_Z2 + 2 * n, d_zp)

    def z_high(n, first):
        high = half_rows(zn, first, 1)
        got(high, I_Z1 + 4 * n + 3)
        send(high, high, I_Z2 + 2 * n + 1, d_zm)

    def z_rest(n, first):
        got(half_rows(zn, first, 0), I_Z1 + 4 * n + 1)
        got(half_rows(zb, first, 1), I_Z1 + 4 * n + 2)

    def to_core(zz, i):
        mine = place(zz, c, 0, 2)
        send(mine, mine, I_CORE + i, d_c)

    def from_y(h):
        near = half_rows(z, 1 - yl, h)
        got(near, I_YL + h)
        send(near, near, I_Z1 + 4 + 2 * h, d_zp)
        send(near, near, I_Z1 + 4 + 2 * h + 1, d_zm)

    def send_y(n, carry):
        send(zc.at[packed(yh), cols(n)], zc.at[packed(yh), cols(n)], Z_Y + n, d_y)
        return carry

    from_y(0)
    lax.fori_loop(0, 2, send_y, 0)
    z_low(0, yl)

    a_grad = jnp.where(act[0].astype(F32) > 0, a_back[...], 0.0).astype(BF16)
    part = nn(gin_in[...].astype(F32).T.astype(BF16), a_grad).astype(BF16)
    for i in range(2):
        for j in range(2):
            r = (i * 2 + j) * 128
            gpart[i, j, :, H:] = part[r:r + 128]
    send(gpart.at[:, 1 - xp, :, pl.ds(H, GH)], gr1.at[:, :, pl.ds(H, GH)], G_E1 + 8, d_e1)
    gint[...] = nt(ga[...], a_grad)
    scen = nt(a_grad, ga[UD:, :])
    tsend[0, :32] = lax.dot_general(
        onehot_t, scen, (((1,), (0,)), ((), ())), precision=lax.Precision.HIGHEST, preferred_element_type=F32)
    over = jnp.maximum(jnp.sum(mask_row, axis=1, keepdims=True) - CAP, 0.0)
    tsend[0, 32:] = jnp.broadcast_to(over, (8, 128))
    t_partners = (d_c, dev(yh, x, yl, z0, c), dev(yh, x, yl, 3 - z, c), d_e1, d_e0, d_yl, d_y)
    send(tsend.at[0], trecv.at[0], T_ALL, t_partners[0])

    def user_rows(t):
        rows = gint[pl.ds(pl.multiple_of(t * USER, 8), USER), :]
        return jnp.concatenate([rows, jnp.zeros((XB - 256 - USER, ROWS), F32)], axis=0).astype(BF16)

    from_y(1)

    lax.fori_loop(2, STEPS, send_y, 0)
    to_core(z, 0)
    z_high(0, yl)

    def x_block(k, carry):
        wcopy(k).wait()
        wrows = wbuf.at[k % 2]
        other = 1 - c
        xsend[k, :256, :] = nt(wrows[pl.ds(pl.multiple_of(other * 256, 256), 256), :], zfull[...]).astype(BF16)
        xsend[k, 256:, :] = user_rows(k * 2 + other)
        send(xsend.at[k], xcore.at[k], X_CORE + k, d_c)
        xkeep[k, :256, :] = nt(wrows[pl.ds(pl.multiple_of(c * 256, 256), 256), :], zfull[...]).astype(BF16)
        xkeep[k, 256:, :] = user_rows(k * 2 + c)

        @pl.when(k < STEPS - 2)
        def _():
            wcopy(k + 2).start()

        return carry

    def inputs_z2():
        for n, first in enumerate((yl, 1 - yl)):
            got(half_rows(zf, first, 0), I_Z2 + 2 * n)
            got(half_rows(zf, first, 1), I_Z2 + 2 * n + 1)
        to_core(zf, 3)

    def forward(k):
        cc = cols(k)
        got(zc.at[packed(1 - yh), cc], Z_Y + k)
        send(zc.at[packed(1 - yh), cc], zc.at[packed(3 - yh), cc], Z_FW + k, d_e0)

        @pl.when(jnp.logical_and(k >= 2, k < 6))
        def _():
            send_e0(k + 2)

    def table_step(s):
        got(trecv.at[s - 1], T_ALL + s - 1)
        tsend[s] = tsend[s - 1] + trecv[s - 1]
        send(tsend.at[s], trecv.at[s], T_ALL + s, t_partners[s])

    def wait_inputs():
        for i, zz in enumerate((z, zb, zn, zf)):
            got(place(zz, 1 - c, 0, 2), I_CORE + i)
        got(sel.at[1 - yh], S_ALL)
        got(sel.at[2 + yh], S_ALL + 1)
        got(sel.at[3 - yh], S_ALL + 2)

    def pack_inputs(d_):
        for s in range(4):
            p = picker(s)
            for j in range(2):
                ac[d_, j, :, s * CAP:(s + 1) * CAP] = nt(
                    aall[d_, j, :, s * ROWS:(s + 1) * ROWS], p).astype(BF16)

    def core_sum():
        def one(n, carry):
            got(xcore.at[n], X_CORE + n)
            xkeep[n] = (xkeep[n].astype(F32) + xcore[n].astype(F32)).astype(BF16)
            return carry

        lax.fori_loop(0, STEPS, one, 0)
        send(xkeep.at[zf], xz1.at[0], X_Z1, d_zp)
        send(xkeep.at[4 + zf], xz1.at[1], X_Z1 + 1, d_zm)

    def gate_e1():
        for n in range(STEPS):
            got(gr1.at[:, :, pl.ds(n * CH, CH)], G_E1 + n)
        got(gr1.at[:, :, pl.ds(H, GH)], G_E1 + 8)
        gpart[1 - yh, xp] = (gpart[1 - yh, xp].astype(F32) + gr1[1 - yh].astype(F32)).astype(BF16)
        send(gpart.at[1 - yh, xp], gr2, G_Y, d_y)

    def gate_y():
        got(gr2, G_Y)
        gpart[yh, xp] = (
            gpart[yh, xp].astype(F32) + gr1[yh].astype(F32) + gr2[...].astype(F32)).astype(BF16)
        far = pl.ds(pl.multiple_of((x0 % 2) * 64, 64), 64)
        send(gpart.at[yh, xp, far], gr3, G_E0, d_e0)

    def gate_e0():
        got(gr3, G_E0)
        near = pl.ds(pl.multiple_of((x % 2) * 64, 64), 64)
        total = gpart[yh, xp, near, :].astype(F32) + gr3[...].astype(F32)
        gb_out[...] = total[:, :H].astype(BF16)
        ga_out[...] = total[:, H:].astype(BF16)

    def x_z1():
        got(xz1.at[0], X_Z1)
        got(xz1.at[1], X_Z1 + 1)
        xkeep[zn] = (xkeep[zn].astype(F32) + xz1[0].astype(F32)).astype(BF16)
        xkeep[4 + zb] = (xkeep[4 + zb].astype(F32) + xz1[1].astype(F32)).astype(BF16)
        for h in range(2):
            send(xkeep.at[h * 4 + zn], xz2.at[0, h], X_Z2 + 2 * h, d_zp)
            send(xkeep.at[h * 4 + zb], xz2.at[1, h], X_Z2 + 1 + 2 * h, d_zm)

    def x_z2():
        for h in range(2):
            got(xz2.at[0, h], X_Z2 + 2 * h)
            got(xz2.at[1, h], X_Z2 + 1 + 2 * h)
        xylsend[...] = (
            xkeep[(1 - yl) * 4 + z].astype(F32) + xz2[0, 1 - yl].astype(F32) + xz2[1, 1 - yl].astype(F32)
        ).astype(BF16)
        send(xylsend, xyl, X_YL, d_yl)

    def x_last():
        got(xyl, X_YL)
        total = (
            xkeep[yl * 4 + z].astype(F32) + xz2[0, yl].astype(F32) + xz2[1, yl].astype(F32)
            + xyl[...].astype(F32))
        x_out[...] = total[:256].T.astype(BF16)
        user_out[...] = total[256:256 + USER].astype(BF16)

    def table_last():
        got(trecv.at[6], T_ALL + 6)
        total = tsend[6] + trecv[6]
        table_out[...] = total[:32]
        flag_out[0, 0] = total[32, 0]

    def table_at(s):
        return lambda: table_step(s)

    extra = {
        1: (table_at(1),),
        2: (table_at(2),),
        3: (table_at(3),),
        4: (core_sum, lambda: pack_inputs(1)),
        5: (gate_e1,),
        6: (x_z1, table_at(4)),
        8: (table_at(5),),
        9: (x_z2, gate_y, table_at(6)),
        11: (x_last, gate_e0, table_last),
    }

    def main_copy(n):
        return pltpu.make_async_copy(main_v.at[:, cols(n)], main_out.at[:, cols(n)], lsem.at[9 + n])

    def step(i, carry):
        j = i - LAG

        @pl.when(i == 1)
        def _():
            def x_and_forward(n, carry):
                forward(n)
                x_block(n + 2, carry)
                return carry

            lax.fori_loop(0, 2, x_and_forward, 0)
            inputs_z2()
            forward(2)

        @pl.when(i == LAG)
        def _():
            wait_inputs()
            pack_inputs(0)

        @pl.when(jnp.logical_and(j >= 0, j < STEPS))
        def _():
            cc = cols(j)
            got(zc.at[packed(2 + yh), cc], Z_E0 + j)
            got(zc.at[packed(3 - yh), cc], Z_FW + j)
            for h in range(2):
                ps[h * 256:(h + 1) * 256, cc] = nn(ac[0, h], zc[:, cc]).astype(BF16)
            send(ps.at[:, cc], pr.at[:, cc], M_E1 + j, d_e1)

        @pl.when(jnp.logical_and(i >= 2, i < 5))
        def _():
            @pl.when(i > 2)
            def _():
                forward(2 * i - 2)

            forward(2 * i - 1)

        @pl.when(jnp.logical_and(i < 4, i != 1))
        def _():
            lax.fori_loop(2 * i, 2 * i + 2, x_block, 0)

        @pl.when(i == 0)
        def _():
            z_low(1, 1 - yl)
            z_high(1, 1 - yl)
            for n, first in enumerate((yl, 1 - yl)):
                z_rest(n, first)
            to_core(zb, 1)
            to_core(zn, 2)

        for at, calls in extra.items():

            @pl.when(i == at)
            def _():
                for call in calls:
                    call()

        @pl.when(j >= AHEAD)
        def _():
            cc = cols(j - AHEAD)
            got(pr.at[:, cc], M_E1 + j - AHEAD)
            for h in range(2):
                total = pr[h * 256:(h + 1) * 256, cc].astype(F32) + nn(ac[1, h], zc[:, cc])
                main_v[h * 256:(h + 1) * 256, cc] = total.astype(BF16)
            main_copy(j - AHEAD).start()

        return carry

    lax.fori_loop(0, STEPS + LAG + AHEAD, step, 0)

    def drain(k, carry):
        cc = cols(k)
        main_copy(k).wait()
        sent(zc.at[packed(0), cc], Z_Y + k)
        sent(zc.at[packed(0), cc], Z_E0 + k)
        sent(zc.at[packed(0), cc], Z_FW + k)
        sent(gr1.at[:, :, cc], G_E1 + k)
        sent(ps.at[:, cc], M_E1 + k)
        sent(xsend.at[k], X_CORE + k)
        return carry

    lax.fori_loop(0, STEPS, drain, 0)
    sent(gr1.at[:, :, pl.ds(H, GH)], G_E1 + 8)
    sent(gr2, G_Y)
    sent(gr3, G_E0)

    @pl.when(jnp.logical_not(stays))
    def _():
        for h in range(2):
            sent(x_own.at[halves[h]], I_PERM + h)

    @pl.when(jnp.logical_and(moved, turn))
    def _():
        for h in range(2):
            sent(x_own.at[halves[h]], I_WAY + h)

    for i in range(2):
        sent(half_rows(z, 0, 0), I_YL + i)
    for i in range(8):
        sent(half_rows(z, 0, 0), I_Z1 + i)
    for i in range(4):
        sent(half_rows(z, 0, 0), I_Z2 + i)
    for i in range(2):
        sent(xz1.at[i], X_Z1 + i)
    for i in range(3):
        sent(sel.at[0], S_ALL + i)
    for i in range(4):
        sent(place(z, c, 0, 2), I_CORE + i)
        sent(xz2.at[0, 0], X_Z2 + i)
    sent(xyl, X_YL)
    for s in range(7):
        sent(tsend.at[s], T_ALL + s)


def copy_kernel(n, *refs):
    held, into, out = refs[2 * n:3 * n], refs[3 * n], refs[3 * n + 1]
    parts = [(i, slice(None)) for i in range(1, n)]
    parts += [(0, pl.ds(r, 64)) for r in range(0, 512, 64)]
    first = [pltpu.make_async_copy(refs[i].at[r], held[i].at[r], into.at[p]) for p, (i, r) in enumerate(parts)]
    second = [pltpu.make_async_copy(held[i].at[r], refs[n + i].at[r], out.at[p]) for p, (i, r) in enumerate(parts)]
    for copy in first:
        copy.start()
    for one, two in zip(first, second):
        one.wait()
        two.start()
    for copy in second:
        copy.wait()


def copy_out(*arrays):
    hbm = pl.BlockSpec(memory_space=pl.ANY)
    n = len(arrays)
    return pl.pallas_call(
        functools.partial(copy_kernel, n),
        out_shape=tuple(jax.ShapeDtypeStruct(a.shape, a.dtype) for a in arrays),
        in_specs=[hbm] * n,
        out_specs=(hbm,) * n,
        scratch_shapes=[pltpu.VMEM(a.shape, a.dtype) for a in arrays]
        + [pltpu.SemaphoreType.DMA((n + 7,)), pltpu.SemaphoreType.DMA((n + 7,))],
    )(*arrays)


def main_grad_wide(
    x_quant, x_scale, user_feats, scenario_ids, scenario_table, label_mask, saved_z, out_grad, gate_a, gate_b,
):
    onehot = (scenario_ids[:, None] == jnp.arange(32, dtype=jnp.int32)[None, :]).astype(BF16)
    scen_rows = jnp.dot(onehot, scenario_table, preferred_element_type=F32).astype(BF16)
    gate_in = jnp.concatenate([user_feats, scen_rows], axis=1)
    a_act = jnp.maximum(jnp.dot(gate_in, gate_a[0], preferred_element_type=F32), 0.0).astype(BF16)
    gate = 2.0 * jax.nn.sigmoid(jnp.dot(a_act, gate_b[0], preferred_element_type=F32))
    masked = out_grad[0].astype(F32) * label_mask.astype(F32)
    z_grad = (masked * gate * (saved_z[0] > 0)).astype(BF16)
    blocks = x_scale.shape[1]
    own = (
        x_quant.astype(F32).reshape(ROWS, blocks, -1) * x_scale.astype(F32)[:, :, None]
    ).reshape(ROWS, -1).astype(BF16)
    inputs = lax.all_to_all(jnp.broadcast_to(own, (16, *own.shape)), "task", 0, 0)
    partial = jnp.einsum("trd,rh->tdh", inputs, z_grad, preferred_element_type=F32).astype(BF16)
    parts = lax.all_to_all(partial.reshape(8, 512, H), "batch", 0, 0)
    return jnp.sum(parts.astype(F32), axis=0).astype(BF16)


def body(
    x_quant, x_scale, user_feats, scenario_ids, scenario_table, label_mask,
    saved_z, out_grad, main_weight, gate_a, gate_b,
):
    vmem = pl.BlockSpec(memory_space=pltpu.VMEM)
    hbm = pl.BlockSpec(memory_space=pl.ANY)
    outs = pl.pallas_call(
        kernel,
        out_shape=(
            jax.ShapeDtypeStruct((512, H), BF16),
            jax.ShapeDtypeStruct((64, GH), BF16),
            jax.ShapeDtypeStruct((64, H), BF16),
            jax.ShapeDtypeStruct((ROWS, 256), BF16),
            jax.ShapeDtypeStruct((USER, ROWS), BF16),
            jax.ShapeDtypeStruct((32, 128), F32),
            jax.ShapeDtypeStruct((1, 1), F32),
        ),
        in_specs=[vmem] * 4 + [hbm] * 7,
        out_specs=(hbm,) + (vmem,) * 5 + (pl.BlockSpec(memory_space=pltpu.SMEM),),
        scratch_shapes=[
            pltpu.VMEM((ROWS, 256), BF16),
            pltpu.VMEM((ROWS, UD), BF16),
            pltpu.VMEM((GH, GH), BF16),
            pltpu.VMEM((GH, H), BF16),
            pltpu.VMEM((ROWS, H), BF16),
            pltpu.VMEM((ROWS, H), BF16),
            pltpu.VMEM((2, 512, H), BF16),
            pltpu.VMEM((ROWS, H), BF16),
            pltpu.VMEM((DEPTH, H), BF16),
            pltpu.VMEM((ROWS, GH), BF16),
            pltpu.VMEM((2, ROWS, GH), BF16),
            pltpu.VMEM((ROWS, GH), F32),
            pltpu.VMEM((512, ROWS), F32),
            pltpu.VMEM((2, 2, 256, 4 * ROWS), BF16),
            pltpu.VMEM((2, 2, 256, DEPTH), BF16),
            pltpu.VMEM((256, ROWS), BF16),
            pltpu.VMEM((256, ROWS), BF16),
            pltpu.VMEM((CAP, ROWS), BF16),
            pltpu.VMEM((4, 8, ROWS), F32),
            pltpu.VMEM((2, 2, 128, H + GH), BF16),
            pltpu.VMEM((2, 128, H + GH), BF16),
            pltpu.VMEM((128, H + GH), BF16),
            pltpu.VMEM((64, H + GH), BF16),
            pltpu.VMEM((8, XB, ROWS), BF16),
            pltpu.VMEM((8, XB, ROWS), BF16),
            pltpu.VMEM((8, XB, ROWS), BF16),
            pltpu.VMEM((2, XB, ROWS), BF16),
            pltpu.VMEM((2, 2, XB, ROWS), BF16),
            pltpu.VMEM((XB, ROWS), BF16),
            pltpu.VMEM((XB, ROWS), BF16),
            pltpu.VMEM((512, H), BF16),
            pltpu.VMEM((512, H), BF16),
            pltpu.VMEM((512, H), BF16),
            pltpu.VMEM((7, 40, 128), F32),
            pltpu.VMEM((7, 40, 128), F32),
            pltpu.SemaphoreType.DMA((9 + STEPS,)),
            pltpu.SemaphoreType.DMA((N_SEM,)),
            pltpu.SemaphoreType.DMA((N_SEM,)),
        ],
        compiler_params=pltpu.CompilerParams(
            collective_id=0, has_side_effects=True, vmem_limit_bytes=60 * 1024 * 1024),
        cost_estimate=pl.CostEstimate(flops=21_000_000_000, bytes_accessed=28_000_000, transcendentals=1_000_000),
    )(
        x_scale.T, scenario_ids[None, :], scenario_table, label_mask.T, x_quant, user_feats, gate_a[0], gate_b[0],
        saved_z[0], out_grad[0], main_weight[0],
    )
    main, grad_a, grad_b, x_grad, user, table_grad = copy_out(*outs[:6])
    args = (
        x_quant, x_scale, user_feats, scenario_ids, scenario_table, label_mask, saved_z, out_grad, gate_a, gate_b)
    _, main = lax.while_loop(
        lambda carry: carry[0] > 0,
        lambda carry: (jnp.zeros_like(carry[0]), main_grad_wide(*args)),
        (outs[6][0, 0], main))
    return main[None], grad_a[None], grad_b[None], x_grad, user.T, table_grad


def solution(mesh):
    placed = (
        P("batch", "task"),
        P("batch", "task"),
        P("batch", None),
        P("batch"),
        P(),
        P("batch", "task"),
        P("task", "batch", None),
        P("task", "batch", None),
        P("task", None, None),
        P("task", None, None),
        P("task", None, None),
    )
    return jax.shard_map(
        body,
        mesh=mesh,
        in_specs=placed,
        out_specs=(
            P("task", "batch", None),
            P("task", "batch", None),
            P("task", "batch", None),
            P("batch", "task"),
            P("batch", "task"),
            P(),
        ),
        check_vma=False,
    )
```
